256 devices in a mesh: seq: 64 (over y_lo, z, x), head: 4 (over y_hi, core).
Axes of the slice: x: 4, y: 4 (y_hi: 2, y_lo: 2; y = y_hi * 2 + y_lo), z: 8, core: 2. Of those that a mesh axis runs over, the one named last changes fastest.
Arguments:
- tokens: bfloat16 [24576, 1280], P('seq'), may hold values from -20 to 20
- w_qkv: bfloat16 [1280, 3, 1280], P(None, None, 'head'), may hold values from -0.15625 to 0.15625
- w_out: bfloat16 [1280, 1280], P('head'), may hold values from -0.15625 to 0.15625
- cotangent: bfloat16 [24576, 1280], P('seq'), may hold values from -16 to 16
- block_mask: int32 [192, 192], P('seq'), may hold values from 0 to 1, as said below
- regions: int32 [24576], P('seq'), may hold values from 0 to 3
Outputs:
- mixed: bfloat16 [24576, 1280], P('seq', 'head')
- grad_tokens: bfloat16 [24576, 1280], P('seq', 'head')
- grad_qkv: float32 [1280, 3, 1280], P('seq', None, 'head')
- grad_out: float32 [1280, 1280], P('head', 'seq')
The draws below stay inside these ranges and needn't reach their ends.
Inputs may be any that keep to these rules, and one draw needn't show every extreme that they name: block_mask is 0 for every block pair whose token ranges of 384 lie more than 3 ranges apart on the closed loop of ranges; pairs exactly 3 ranges apart are 1 in some block of every range.
All inputs are finite; a program needn't handle non-finite values.
Results may differ from the reference program's by a relative error of at most 0.02.
Values may be sent and summed in bfloat16 or wider, within the bound.
No kernel may reach another device: no remote copies, remote signals or barrier semaphores. Data moves between devices by JAX's collectives and lax.ppermute only.
A program may use at most 128 MiB of HBM per device.

```python
import jax
import jax.numpy as jnp
from jax import lax

D = 1280
H = 16
HD = 80
TOK_DEV = 384
BLOCK = 128
SPAN = 3
REGIONS = 4
TOKENS = 24576
NB = 192
N_SEQ = 64


def draw_tokens(key, part):
    key = jax.random.fold_in(key, 11)
    first = jax.random.fold_in(key, 0)
    values = jnp.clip(jax.random.normal(first, (TOKENS, D), jnp.float32), -6.0, 6.0)
    return values.astype(jnp.bfloat16)


def draw_block_mask(key, part):
    key = jax.random.fold_in(key, 23)
    first, second = jax.random.split(key)
    per_range = TOK_DEV // BLOCK
    ranges = NB // per_range
    blocks = jnp.arange(NB, dtype=jnp.int32)
    owner = blocks // per_range
    apart = jnp.abs(owner[:, None] - owner[None, :])
    apart = jnp.minimum(apart, ranges - apart)
    levels = jax.random.randint(first, (ranges,), 10, 90)
    rolls = jax.random.randint(second, (NB, NB), 0, 100)
    picked = rolls < levels[owner][:, None]
    leading = blocks % per_range == 0
    forced = (apart == SPAN) & leading[:, None] & leading[None, :]
    return ((apart <= SPAN) & (picked | forced)).astype(jnp.int32)


def touch_ends(drawn, key, least, top_value):
    index_at = [jax.random.randint(jax.random.fold_in(key, axis), (), 0, length) for axis, length in enumerate(drawn.shape)]
    widest = drawn.shape.index(max(drawn.shape))
    next_to = index_at[:widest] + [(index_at[widest] + 1) % drawn.shape[widest]] + index_at[widest + 1:]
    return drawn.at[tuple(index_at)].set(least).at[tuple(next_to)].set(top_value)


def raised(array, rng, source, target, shards_of, factor):
    def block_of(axis_at):
        return (jnp.arange(array.shape[axis_at]) // (array.shape[axis_at] // shards_of)).reshape((-1,) + (1,) * (array.ndim - 1 - axis_at))

    one_side = jax.random.permutation(rng, shards_of)[block_of(target)]
    other_side = (block_of(target) + shards_of // 2) % shards_of
    return jnp.where((block_of(source) == one_side) | (block_of(source) == other_side), factor * array, array)


def shard_levels(rng, shape, pieces, smallest, top_value):
    def one(position, blocks):
        heights = jax.random.uniform(jax.random.fold_in(jax.random.fold_in(rng, 6), position), (blocks,), jnp.float32, smallest / len(pieces), top_value / len(pieces))
        return jnp.repeat(jnp.exp(heights), shape[position] // blocks).reshape((-1,) + (1,) * (len(shape) - position - 1))

    factor_of = one(*pieces[0])
    for cut in pieces[1:]:
        factor_of = factor_of * one(*cut)
    return factor_of


def scatter_about(rng, shape, spread, bound, cuts=(), held_as=jnp.bfloat16):
    factor_of = shard_levels(rng, shape, cuts, -0.22, 0.18) if cuts else 1.0
    values = jax.random.normal(rng, shape, jnp.float32) * spread * factor_of
    return jnp.minimum(jnp.maximum(values, -bound), bound).astype(held_as)


def heavy_noise(own_key, extent, scale, reach, pieces, heavy, kind=jnp.bfloat16):
    drawn = scale * jax.random.normal(own_key, extent, jnp.float32)
    if pieces:
        drawn = drawn * shard_levels(own_key, extent, pieces, -0.22, 0.18)
    return jnp.clip(raised(drawn, jax.random.fold_in(own_key, 3), *heavy), -reach, reach).astype(kind)


def setup_inputs(seed: int = 0) -> dict:
    key_list = jax.random.split(jax.random.key(seed), 7)
    return {
        "tokens": draw_tokens(jax.random.fold_in(key_list[6], 71), 0),
        "w_qkv": scatter_about(key_list[1], (D, 3, D), D ** -0.5, 0.15625, ((2, 4),)),
        "w_out": scatter_about(key_list[2], (D, D), D ** -0.5, 0.15625, ((0, 4),)),
        "cotangent": heavy_noise(key_list[3], (TOKENS, D), 1.0, 16.0, ((0, 64),), (0, 1, 64, 4.0)),
        "block_mask": draw_block_mask(jax.random.fold_in(key_list[6], 71), 0),
        "regions": touch_ends(jax.random.randint(key_list[5], (TOKENS,), 0, REGIONS), jax.random.fold_in(key_list[5], 1), 0, REGIONS - 1).astype(jnp.int32),
    }


def key_rows(stretch):
    offsets = jnp.arange(-SPAN, SPAN + 1, dtype=jnp.int32)
    sources = (stretch + offsets) % N_SEQ
    inner = jnp.arange(TOK_DEV, dtype=jnp.int32)
    return (sources[:, None] * TOK_DEV + inner[None, :]).reshape(-1)


def allowed(stretch, block_mask, regions):
    rows = stretch * TOK_DEV + jnp.arange(TOK_DEV, dtype=jnp.int32)
    cols = key_rows(stretch)
    query_block = rows // BLOCK
    key_block = cols // BLOCK
    bits = block_mask[query_block][:, key_block]
    near = (bits > 0) | (query_block[:, None] == key_block[None, :])
    return rows, cols, near & (regions[rows][:, None] == regions[cols][None, :])


def probabilities(query, key, rows, cols, allow):
    scale = HD ** -0.5
    q_rows = query[rows].astype(jnp.float32)
    k_rows = key[cols].astype(jnp.float32)
    scores = jnp.einsum("qhd,khd->hqk", q_rows, k_rows) * scale
    scores = jnp.where(allow[None], scores, -jnp.inf)
    top = jnp.max(scores, axis=2, keepdims=True)
    expo = jnp.exp(scores - top)
    return (expo / jnp.sum(expo, axis=2, keepdims=True)).astype(jnp.bfloat16)


def reference(tokens, w_qkv, w_out, cotangent, block_mask, regions):
    total = tokens.shape[0]
    flat_w = w_qkv.reshape(D, 3 * D)
    packed = jnp.dot(tokens, flat_w, preferred_element_type=jnp.float32).astype(jnp.bfloat16)
    query = packed[:, :D].reshape(total, H, HD)
    key = packed[:, D:2 * D].reshape(total, H, HD)
    value = packed[:, 2 * D:].reshape(total, H, HD)
    scale = HD ** -0.5
    stretches = jnp.arange(N_SEQ, dtype=jnp.int32)

    def forward_stretch(stretch):
        rows, cols, allow = allowed(stretch, block_mask, regions)
        probs = probabilities(query, key, rows, cols, allow)
        probs32 = lax.optimization_barrier(probs).astype(jnp.float32)
        return jnp.einsum("hqk,khd->qhd", probs32, value[cols].astype(jnp.float32)).astype(jnp.bfloat16)

    attn = lax.map(forward_stretch, stretches).reshape(total, D)
    mixed = jnp.dot(attn, w_out, preferred_element_type=jnp.float32).astype(jnp.bfloat16)
    d_attn = jnp.dot(cotangent, w_out.T, preferred_element_type=jnp.float32).astype(jnp.bfloat16)
    grad_out = jnp.dot(attn.T, cotangent, preferred_element_type=jnp.float32) * (TOKENS ** -0.5)
    d_attn_h = d_attn.reshape(total, H, HD)
    attn_h = attn.reshape(total, H, HD)

    def backward_stretch(carry, stretch):
        d_key, d_value = carry
        rows, cols, allow = allowed(stretch, block_mask, regions)
        probs = probabilities(query, key, rows, cols, allow)
        probs32 = lax.optimization_barrier(probs).astype(jnp.float32)
        grad_rows = d_attn_h[rows].astype(jnp.float32)
        delta = jnp.sum(grad_rows * attn_h[rows].astype(jnp.float32), axis=2).T[:, :, None]
        d_probs = jnp.einsum("qhd,khd->hqk", grad_rows, value[cols].astype(jnp.float32))
        d_scores = (probs32 * (d_probs - delta) * scale).astype(jnp.bfloat16)
        d_scores = lax.optimization_barrier(d_scores).astype(jnp.float32)
        d_query = jnp.einsum("hqk,khd->qhd", d_scores, key[cols].astype(jnp.float32))
        key_part = jnp.einsum("hqk,qhd->khd", d_scores, query[rows].astype(jnp.float32))
        value_part = jnp.einsum("hqk,qhd->khd", probs32, grad_rows)
        d_key = d_key.at[cols].add(key_part)
        d_value = d_value.at[cols].add(value_part)
        return (d_key, d_value), d_query.astype(jnp.bfloat16)

    start = jnp.zeros((total, H, HD), jnp.float32)
    (d_key, d_value), d_query = lax.scan(backward_stretch, (start, start), stretches)
    d_packed = jnp.concatenate([d_query.reshape(total, D), d_key.reshape(total, D).astype(jnp.bfloat16), d_value.reshape(total, D).astype(jnp.bfloat16)], axis=1)
    grad_tokens = jnp.dot(d_packed, flat_w.T, preferred_element_type=jnp.float32).astype(jnp.bfloat16)
    grad_qkv = (jnp.dot(tokens.T, d_packed, preferred_element_type=jnp.float32) * (TOKENS ** -0.5)).reshape(D, 3, D)
    return mixed, grad_tokens, grad_qkv, grad_out
```

```python
import functools

import jax
import jax.numpy as jnp
from jax import lax
from jax.experimental import pallas as pl
from jax.experimental.pallas import tpu as pltpu
from jax.sharding import Mesh
from jax.sharding import PartitionSpec as P

HD = 80
BLOCK = 128
SPAN = 3
TOK = 384
GROUP = 4
PIECES = GROUP + 2 * SPAN
WINDOW = 2 * SPAN + 1
ROW = GROUP * TOK
HALO = SPAN * TOK
KEYS = PIECES * TOK
ROWS = 16
NB = 192
SCALE = HD ** (-0.5)
LOG2E = 1.4426950408889634
NEG = -1e30
BF = jnp.bfloat16
F32 = jnp.float32
VMEM_LIMIT = 48 * 1024 * 1024
ROW_AXES = ("y", "z")
SEQ_AXES = ("y", "z", "x")
HEAD_AXES = ("h", "c")


def shift(value, axis, steps):
    count = lax.axis_size(axis)
    return lax.ppermute(value, axis, [(i, (i + steps) % count) for i in range(count)])


def spec_vmem():
    return pl.BlockSpec(memory_space=pltpu.VMEM)


def spec_smem():
    return pl.BlockSpec(memory_space=pltpu.SMEM)


def call(kernel, outs, ins, scratch=(), flops=0, moved=0, exps=0):
    return pl.pallas_call(
        kernel,
        out_shape=[jax.ShapeDtypeStruct(s, d) for s, d in outs],
        in_specs=[spec_smem()] + [spec_vmem()] * (len(ins) - 1),
        out_specs=[spec_vmem()] * len(outs),
        scratch_shapes=list(scratch),
        compiler_params=pltpu.CompilerParams(vmem_limit_bytes=VMEM_LIMIT),
        cost_estimate=pl.CostEstimate(flops=flops, bytes_accessed=moved, transcendentals=exps),
    )(*ins)


def dot_nn(a, b):
    return lax.dot_general(a, b, (((1,), (0,)), ((), ())), preferred_element_type=F32)


def dot_nt(a, b):
    return lax.dot_general(a, b, (((1,), (1,)), ((), ())), preferred_element_type=F32)


def project_kernel(place, w, tokens, extra, *outs):
    x = place[1]
    for k in range(GROUP):
        head = lax.rem(x + k, GROUP)
        for part in range(3):
            piece = dot_nt(w[part, head], tokens[...])
            outs[k][part * HD : (part + 1) * HD, :] = piece.astype(BF)
        outs[k][3 * HD :, :] = extra[...]


def project_grad_kernel(place, w, cotangent, *outs):
    x = place[1]
    for k in range(GROUP):
        head = lax.rem(x + k, GROUP)
        outs[k][...] = dot_nt(w[head], cotangent[...]).astype(BF)


def halo_kernel(place, r0, r1, r2, r3, to_next, to_prev):
    x = place[1]
    for k, ref in enumerate((r0, r1, r2, r3)):
        pos = lax.rem(x - k + GROUP, GROUP)

        @pl.when(pos >= 1)
        def _():
            at = pl.multiple_of((pos - 1) * TOK, TOK)
            to_next[:, pl.ds(at, TOK)] = ref[HD:, :]

        @pl.when(pos <= 2)
        def _():
            at = pl.multiple_of(pos * TOK, TOK)
            to_prev[:, pl.ds(at, TOK)] = ref[HD:, :]


def attention_kernel(place, r0, r1, r2, r3, d0, d1, d2, d3, from_prev, from_next,
                     attn, dq, gp, gn, own, a0, a1, a2, a3, q0, q1, q2, q3,
                     kt, vt, reg, eff, qt, dot_, s_ref, p_ref, ds_ref, dk, dv):
    row = place[0]
    x = place[1]
    kt[:, :HALO] = from_prev[:HD, :]
    vt[:, :HALO] = from_prev[HD : 2 * HD, :]
    reg[:, :HALO] = from_prev[2 * HD :, :].astype(F32)
    kt[:, HALO + ROW :] = from_next[:HD, :]
    vt[:, HALO + ROW :] = from_next[HD : 2 * HD, :]
    reg[:, HALO + ROW :] = from_next[2 * HD :, :].astype(F32)
    block_of = lax.broadcasted_iota(jnp.int32, (256, KEYS), 1) // BLOCK
    block_id = lax.rem(block_of + row * (ROW // BLOCK) - HALO // BLOCK + NB, NB)
    pick = jnp.where(block_id == lax.broadcasted_iota(jnp.int32, (256, KEYS), 0), 1.0, 0.0).astype(BF)
    for k, (ref, grad) in enumerate(((r0, d0), (r1, d1), (r2, d2), (r3, d3))):
        pos = lax.rem(x - k + GROUP, GROUP)
        at = pl.multiple_of(HALO + pos * TOK, TOK)
        kt[:, pl.ds(at, TOK)] = ref[HD : 2 * HD, :]
        vt[:, pl.ds(at, TOK)] = ref[2 * HD : 3 * HD, :]
        reg[:, pl.ds(at, TOK)] = ref[3 * HD :, :].astype(F32)
        eff[pos] = dot_nn(ref[3 * HD :, :256], pick)
        qt[pos] = ref[:HD, :]
        dot_[pos] = grad[...]
    dk[...] = jnp.zeros_like(dk)
    dv[...] = jnp.zeros_like(dv)

    def step(r, carry):
        at = pl.multiple_of(r * TOK, TOK)

        def win(c):
            return pl.ds(pl.multiple_of(at + c * TOK, TOK), TOK)

        q_n = qt[r].astype(F32).T.astype(BF)
        do_n = dot_[r].astype(F32).T
        reg_q = reg[:, pl.ds(pl.multiple_of(HALO + at, TOK), TOK)].T[:, 0:1]
        top = [jnp.full((BLOCK, BLOCK), NEG, F32)] * 3
        for c in range(WINDOW):
            raw = dot_nn(q_n, kt[:, win(c)])
            key_reg = reg[0:1, win(c)]
            blocks = lax.broadcasted_iota(jnp.int32, (1, TOK), 1) // BLOCK
            for i in range(3):
                open_ = eff[r, 1 + i : 2 + i, win(c)] > 0.5
                if c == SPAN:
                    open_ = open_ | (blocks == i)
                key_eff = jnp.where(open_, key_reg, -1.0)
                rows = slice(i * BLOCK, (i + 1) * BLOCK)
                s = jnp.where(reg_q[rows] == key_eff, raw[rows], NEG)
                s_ref[rows, c * TOK : (c + 1) * TOK] = s
                for g in range(3):
                    top[i] = jnp.maximum(top[i], s[:, g * BLOCK : (g + 1) * BLOCK])
        m = jnp.concatenate([jnp.max(t, axis=1, keepdims=True) for t in top], axis=0)
        total = jnp.zeros((TOK, BLOCK), F32)
        out = jnp.zeros((TOK, HD), F32)
        for c in range(WINDOW):
            p = jnp.exp2((s_ref[:, c * TOK : (c + 1) * TOK] - m) * (SCALE * LOG2E))
            for g in range(3):
                total = total + p[:, g * BLOCK : (g + 1) * BLOCK]
            pb = p.astype(BF)
            p_ref[:, c * TOK : (c + 1) * TOK] = pb
            out = out + dot_nt(pb, vt[:, win(c)])
        inv = 1.0 / jnp.sum(total, axis=1, keepdims=True)
        at_n = (out * inv).astype(BF).astype(F32)
        dos_n = (do_n * (inv * SCALE)).astype(BF)
        delta = jnp.sum(dos_n.astype(F32) * at_n, axis=1, keepdims=True)
        d_q = jnp.zeros((TOK, HD), F32)
        for c in range(WINDOW):
            cols = slice(c * TOK, (c + 1) * TOK)
            dp = dot_nn(dos_n, vt[:, win(c)])
            ds = (p_ref[:, cols].astype(F32) * (dp - delta)).astype(BF)
            ds_ref[:, cols] = ds
            d_q = d_q + dot_nt(ds, kt[:, win(c)])
        dos_t = dos_n.astype(F32).T.astype(BF)
        for c in range(WINDOW):
            cols = slice(c * TOK, (c + 1) * TOK)
            dk[:, win(c)] += dot_nn(qt[r], ds_ref[:, cols])
            dv[:, win(c)] += dot_nn(dos_t, p_ref[:, cols])
        attn_t = at_n.T.astype(BF)
        dq_t = d_q.T.astype(BF)
        attn[:, pl.ds(at, TOK)] = attn_t
        dq[:, pl.ds(at, TOK)] = dq_t
        k_to = lax.rem(r - x + GROUP, GROUP)
        for k, (a_out, q_out) in enumerate(((a0, q0), (a1, q1), (a2, q2), (a3, q3))):
            @pl.when(k_to == k)
            def _():
                a_out[...] = attn_t
                q_out[...] = dq_t
        return carry

    lax.fori_loop(0, GROUP, step, 0)
    unscale = 1.0 / SCALE
    gp[:HD, :] = dk[:, :HALO].astype(BF)
    gp[HD:, :] = (dv[:, :HALO] * unscale).astype(BF)
    gn[:HD, :] = dk[:, HALO + ROW :].astype(BF)
    gn[HD:, :] = (dv[:, HALO + ROW :] * unscale).astype(BF)
    own[:HD, :] = dk[:, HALO : HALO + ROW]
    own[HD:, :] = dv[:, HALO : HALO + ROW] * unscale


def attention(place, parts, grads, from_prev, from_next):
    chunk = ((HD, TOK), BF)
    outs = [((HD, ROW), BF)] * 2 + [((2 * HD, HALO), BF)] * 2 + [((2 * HD, ROW), F32)] + [chunk] * 8
    scratch = [
        pltpu.VMEM((HD, KEYS), BF),
        pltpu.VMEM((HD, KEYS), BF),
        pltpu.VMEM((16, KEYS), F32),
        pltpu.VMEM((GROUP, 16, KEYS), F32),
        pltpu.VMEM((GROUP, HD, TOK), BF),
        pltpu.VMEM((GROUP, HD, TOK), BF),
        pltpu.VMEM((TOK, WINDOW * TOK), F32),
        pltpu.VMEM((TOK, WINDOW * TOK), BF),
        pltpu.VMEM((TOK, WINDOW * TOK), BF),
        pltpu.VMEM((HD, KEYS), F32),
        pltpu.VMEM((HD, KEYS), F32),
    ]
    return call(
        attention_kernel, outs, [place, *parts, *grads, from_prev, from_next], scratch,
        flops=12 * ROW * WINDOW * TOK * 128, moved=6_000_000, exps=ROW * WINDOW * TOK,
    )


def combine_kernel(place, own, from_next, from_prev, full, c0, c1, c2, c3):
    x = place[1]
    full[:, :TOK] = (own[:, :TOK] + from_prev[:, :TOK].astype(F32)).astype(BF)
    middle = own[:, TOK:HALO] + from_next[:, : HALO - TOK].astype(F32)
    full[:, TOK:HALO] = (middle + from_prev[:, TOK:].astype(F32)).astype(BF)
    full[:, HALO:] = (own[:, HALO:] + from_next[:, HALO - TOK :].astype(F32)).astype(BF)
    for k, out in enumerate((c0, c1, c2, c3)):
        at = pl.multiple_of(lax.rem(x + k, GROUP) * TOK, TOK)
        out[...] = full[:, pl.ds(at, TOK)]


def weights_kernel(scale, half, place, dq, dkv, attn, tokens, cotangent, out):
    left = jnp.concatenate([dq[...], dkv[...]], axis=0)
    term = dot_nn(left, tokens[...]) * scale
    term_out = dot_nn(attn[...], cotangent[...]) * scale
    out[...] = jnp.concatenate([term, term_out], axis=0).T.astype(out.dtype)


def weights_half(scale, place, other, dq, dkv, attn, tokens, cotangent, dtype):
    model = tokens.shape[1]
    per_half = model // 2 // BLOCK

    def columns(j, place):
        y = lax.rem(place[0] // (ROWS // 2) + (1 if other else 0), 2)
        return (0, y * per_half + j)

    whole = lambda a: pl.BlockSpec(a.shape, lambda j, place: (0, 0))
    return pl.pallas_call(
        functools.partial(weights_kernel, scale, other),
        grid_spec=pltpu.PrefetchScalarGridSpec(
            num_scalar_prefetch=1,
            grid=(per_half,),
            in_specs=[whole(dq), whole(dkv), whole(attn)]
            + [pl.BlockSpec((ROW, BLOCK), columns)] * 2,
            out_specs=pl.BlockSpec((BLOCK, 4 * HD), lambda j, place: (j, 0)),
        ),
        out_shape=jax.ShapeDtypeStruct((model // 2, 4 * HD), dtype),
        compiler_params=pltpu.CompilerParams(vmem_limit_bytes=VMEM_LIMIT),
        cost_estimate=pl.CostEstimate(
            flops=2 * 4 * HD * ROW * model // 2, bytes_accessed=5_000_000, transcendentals=0
        ),
    )(place, dq, dkv, attn, tokens, cotangent)


def scatter_heads(weights_send, weights_keep, values):
    width = values.shape[1]
    contract = (((0,), (0,)), ((), ()))
    send = lax.dot_general(weights_send, values, contract, preferred_element_type=F32).astype(BF)
    got = shift(send, "c", 1)
    keep = lax.dot_general(weights_keep, values, contract, preferred_element_type=F32)
    half = (keep + got.astype(F32)).reshape(2, -1, width)
    h = lax.axis_index("h")
    other = lax.dynamic_index_in_dim(half, 1 - h, 0, keepdims=False).astype(BF)
    mine = lax.dynamic_index_in_dim(half, h, 0, keepdims=False)
    return (mine + shift(other, "h", 1).astype(F32)).astype(BF)


def on_device(tokens, w_qkv, w_out, cotangent, block_mask, regions):
    width, model = tokens.shape
    local = w_out.shape[0]
    x = lax.axis_index("x")
    c = lax.axis_index("c")
    row = lax.axis_index("y") * (ROWS // 2) + lax.axis_index("z")
    place = jnp.stack([row, x]).astype(jnp.int32)
    grad_scale = (width * lax.axis_size(SEQ_AXES)) ** (-0.5)
    half = width // 2
    part_of = lambda a: lax.dynamic_slice_in_dim(a, c * half, half, 0)
    tokens_row = lax.all_gather(part_of(tokens), ("x", "c"), axis=0, tiled=True)
    cot_row = lax.all_gather(part_of(cotangent), ("x", "c"), axis=0, tiled=True)

    w3 = w_qkv.transpose(1, 2, 0).reshape(3, GROUP, HD, model)
    w_out4 = w_out.reshape(GROUP, HD, model)
    extra = jnp.concatenate(
        [
            regions[None, :].astype(BF),
            jnp.pad(block_mask.astype(BF), ((0, 0), (0, width - NB))),
            jnp.zeros((12, width), BF),
        ],
        axis=0,
    )
    sent = call(
        project_kernel, [((256, width), BF)] * GROUP, [place, w3, tokens, extra],
        flops=2 * 3 * local * model * width, moved=5_000_000,
    )
    parts = [sent[0]] + [shift(sent[k], "x", k) for k in (1, 2, 3)]
    sent_grad = call(
        project_grad_kernel, [((HD, width), BF)] * GROUP, [place, w_out4, cotangent],
        flops=2 * local * model * width, moved=3_000_000,
    )
    grads = [sent_grad[0]] + [shift(sent_grad[k], "x", k) for k in (1, 2, 3)]
    to_next, to_prev = call(
        halo_kernel, [((2 * HD + 16, HALO), BF)] * 2, [place, *parts], moved=2_000_000
    )
    from_prev = shift(to_next, ROW_AXES, 1)
    from_next = shift(to_prev, ROW_AXES, -1)

    order = [(x - k) % GROUP for k in range(GROUP)]
    w_turned = jnp.concatenate(
        [lax.dynamic_index_in_dim(w3, o, 1, keepdims=False).reshape(3 * HD, model) for o in order]
    )
    w_out_turned = jnp.concatenate(
        [lax.dynamic_index_in_dim(w_out4, o, 0, keepdims=False) for o in order]
    )

    def cut(weights, core):
        cols = weights.reshape(-1, 2, 2, local)
        return lax.dynamic_index_in_dim(cols, core, 2, keepdims=False).reshape(-1, 2 * local)

    cuts = lax.optimization_barrier(
        (cut(w_turned, 1 - c), cut(w_turned, c), cut(w_out_turned, 1 - c), cut(w_out_turned, c))
    )

    attn, dq, gp, gn, own, *chunks = attention(place, parts, grads, from_prev, from_next)
    a_chunks, q_chunks = chunks[:4], chunks[4:]
    back_next = shift(gp, ROW_AXES, -1)
    back_prev = shift(gn, ROW_AXES, 1)
    a_all = [a_chunks[0]] + [shift(a_chunks[k], "x", k) for k in (1, 2, 3)]
    q_all = [q_chunks[0]] + [shift(q_chunks[k], "x", k) for k in (1, 2, 3)]
    mixed_t = scatter_heads(cuts[2], cuts[3], jnp.concatenate(a_all, axis=0))

    dkv, *kv_chunks = call(
        combine_kernel, [((2 * HD, ROW), BF)] + [((2 * HD, width), BF)] * GROUP,
        [place, own, back_next, back_prev], moved=3_000_000,
    )
    kv_all = [kv_chunks[0]] + [shift(kv_chunks[k], "x", k) for k in (1, 2, 3)]
    send_w = weights_half(grad_scale, place, True, dq, dkv, attn, tokens_row, cot_row, BF)
    got_w = shift(send_w, "y", 1)
    keep_w = weights_half(grad_scale, place, False, dq, dkv, attn, tokens_row, cot_row, F32)
    d_packed = jnp.concatenate([a for k in range(GROUP) for a in (q_all[k], kv_all[k])], axis=0)
    grad_tokens_t = scatter_heads(cuts[0], cuts[1], d_packed)

    half_w = (keep_w + got_w.astype(F32)).astype(BF).reshape(ROWS // 2, model // ROWS, 4 * HD)
    spread = lax.all_to_all(half_w, "z", 0, 0, tiled=True)
    summed = jnp.sum(spread.astype(F32), axis=0).reshape(GROUP, -1, 4 * HD)
    final = lax.all_to_all(summed, "x", 0, 0, tiled=True)
    share = final.shape[1]
    final = final.reshape(GROUP, share, 4, HD).transpose(1, 2, 0, 3).reshape(share, 4, local)
    return (mixed_t.T, grad_tokens_t.T, final[:, :3], final[:, 3].T)


def solution(mesh):
    devices = mesh.devices.reshape(2, ROWS // 2, GROUP, 2, 2)
    fine = Mesh(devices, ("y", "z", "x", "h", "c"))
    placed = (
        P(SEQ_AXES, None),
        P(None, None, HEAD_AXES),
        P(HEAD_AXES, None),
        P(SEQ_AXES, None),
        P(SEQ_AXES, None),
        P(SEQ_AXES),
    )
    return jax.shard_map(
        on_device,
        mesh=fine,
        in_specs=placed,
        out_specs=(
            P(SEQ_AXES, HEAD_AXES),
            P(SEQ_AXES, HEAD_AXES),
            P(SEQ_AXES, None, HEAD_AXES),
            P(HEAD_AXES, SEQ_AXES),
        ),
        check_vma=False,
    )
```

```python
import functools

import jax
import jax.numpy as jnp
from jax import lax
from jax.experimental import pallas as pl
from jax.experimental.pallas import tpu as pltpu
from jax.sharding import Mesh
from jax.sharding import PartitionSpec as P

HD = 80
BLOCK = 128
SPAN = 3
TOK = 384
GROUP = 4
PIECES = GROUP + 2 * SPAN
WINDOW = 2 * SPAN + 1
ROW = GROUP * TOK
HALO = SPAN * TOK
KEYS = PIECES * TOK
ROWS = 16
NB = 192
SCALE = HD ** (-0.5)
LOG2E = 1.4426950408889634
NEG = -1e30
BF = jnp.bfloat16
F32 = jnp.float32
VMEM_LIMIT = 48 * 1024 * 1024
ROW_AXES = ("y", "z")
SEQ_AXES = ("y", "z", "x")
HEAD_AXES = ("h", "c")


def shift(value, axis, steps):
    count = lax.axis_size(axis)
    return lax.ppermute(value, axis, [(i, (i + steps) % count) for i in range(count)])


def spec_vmem():
    return pl.BlockSpec(memory_space=pltpu.VMEM)


def spec_smem():
    return pl.BlockSpec(memory_space=pltpu.SMEM)


def call(kernel, outs, ins, scratch=(), flops=0, moved=0, exps=0):
    return pl.pallas_call(
        kernel,
        out_shape=[jax.ShapeDtypeStruct(s, d) for s, d in outs],
        in_specs=[spec_smem()] + [spec_vmem()] * (len(ins) - 1),
        out_specs=[spec_vmem()] * len(outs),
        scratch_shapes=list(scratch),
        compiler_params=pltpu.CompilerParams(vmem_limit_bytes=VMEM_LIMIT),
        cost_estimate=pl.CostEstimate(flops=flops, bytes_accessed=moved, transcendentals=exps),
    )(*ins)


def dot_nn(a, b):
    return lax.dot_general(a, b, (((1,), (0,)), ((), ())), preferred_element_type=F32)


def dot_nt(a, b):
    return lax.dot_general(a, b, (((1,), (1,)), ((), ())), preferred_element_type=F32)


def project_kernel(place, w, tokens, regions, mask, o0, o1, o2, o3, part, extra, held):
    x = place[1]
    extra[...] = jnp.zeros_like(extra)
    extra[0:1, :] = regions[...].astype(F32)
    extra[1:4, :NB] = mask[...].astype(F32)
    for piece in range(3):
        packed = dot_nt(w[piece].reshape(GROUP * HD, -1), tokens[...])
        held[piece] = packed.astype(BF).reshape(GROUP, HD, -1)
    for k, out in enumerate((o0, o1, o2, o3)):
        head = lax.rem(x + k, GROUP)
        for piece in range(3):
            out[piece * HD : (piece + 1) * HD, :] = held[piece, head]
        out[3 * HD :, :] = extra[...].astype(BF)
    half = tokens.shape[0] // 2
    part[...] = tokens[pl.ds(pl.multiple_of(place[3] * half, half), half), :]


def project_grad_kernel(place, w, cotangent, o0, o1, o2, o3, part, held):
    x = place[1]
    held[...] = dot_nt(w[...], cotangent[...]).astype(BF).reshape(GROUP, HD, -1)
    for k, out in enumerate((o0, o1, o2, o3)):
        out[...] = held[lax.rem(x + k, GROUP)]
    half = cotangent.shape[0] // 2
    part[...] = cotangent[pl.ds(pl.multiple_of(place[3] * half, half), half), :]


def turn_kernel(place, w, w_out, wt, w_out_t):
    wt[...] = w[...].T
    w_out_t[...] = w_out[...].T


def halo_kernel(place, r0, r1, r2, r3, to_next, to_prev):
    x = place[1]
    for k, ref in enumerate((r0, r1, r2, r3)):
        pos = lax.rem(x - k + GROUP, GROUP)

        @pl.when(pos >= 1)
        def _():
            at = pl.multiple_of((pos - 1) * TOK, TOK)
            to_next[:, pl.ds(at, TOK)] = ref[HD:, :]

        @pl.when(pos <= 2)
        def _():
            at = pl.multiple_of(pos * TOK, TOK)
            to_prev[:, pl.ds(at, TOK)] = ref[HD:, :]


def attention_kernel(place, r0, r1, r2, r3, d0, d1, d2, d3, from_prev, from_next,
                     early, gp, gn, own, o0, o1, o2, o3,
                     kt, vt, reg, eff, qt, dot_, s_ref, p_ref, ds_ref, dk, dv):
    row = place[0]
    x = place[1]
    kt[:, :HALO] = from_prev[:HD, :]
    vt[:, :HALO] = from_prev[HD : 2 * HD, :]
    reg[:, :HALO] = from_prev[2 * HD :, :].astype(F32)
    kt[:, HALO + ROW :] = from_next[:HD, :]
    vt[:, HALO + ROW :] = from_next[HD : 2 * HD, :]
    reg[:, HALO + ROW :] = from_next[2 * HD :, :].astype(F32)
    block_of = lax.broadcasted_iota(jnp.int32, (256, KEYS), 1) // BLOCK
    block_id = lax.rem(block_of + row * (ROW // BLOCK) - HALO // BLOCK + NB, NB)
    pick = jnp.where(block_id == lax.broadcasted_iota(jnp.int32, (256, KEYS), 0), 1.0, 0.0).astype(BF)
    for k, (ref, grad) in enumerate(((r0, d0), (r1, d1), (r2, d2), (r3, d3))):
        pos = lax.rem(x - k + GROUP, GROUP)
        at = pl.multiple_of(HALO + pos * TOK, TOK)
        kt[:, pl.ds(at, TOK)] = ref[HD : 2 * HD, :]
        vt[:, pl.ds(at, TOK)] = ref[2 * HD : 3 * HD, :]
        reg[:, pl.ds(at, TOK)] = ref[3 * HD :, :].astype(F32)
        eff[pos] = dot_nn(ref[3 * HD :, :256], pick)
        qt[pos] = ref[:HD, :]
        dot_[pos] = grad[...]
    dk[...] = jnp.zeros_like(dk)
    dv[...] = jnp.zeros_like(dv)

    def step(r, carry):
        at = pl.multiple_of(r * TOK, TOK)

        def win(c):
            return pl.ds(pl.multiple_of(at + c * TOK, TOK), TOK)

        q_n = qt[r].astype(F32).T.astype(BF)
        do_n = dot_[r].astype(F32).T
        reg_q = reg[:, pl.ds(pl.multiple_of(HALO + at, TOK), TOK)].T[:, 0:1]
        top = [jnp.full((BLOCK, BLOCK), NEG, F32)] * 3
        for c in range(WINDOW):
            raw = dot_nn(q_n, kt[:, win(c)])
            key_reg = reg[0:1, win(c)]
            blocks = lax.broadcasted_iota(jnp.int32, (1, TOK), 1) // BLOCK
            for i in range(3):
                open_ = eff[r, 1 + i : 2 + i, win(c)] > 0.5
                if c == SPAN:
                    open_ = open_ | (blocks == i)
                key_eff = jnp.where(open_, key_reg, -1.0)
                rows = slice(i * BLOCK, (i + 1) * BLOCK)
                s = jnp.where(reg_q[rows] == key_eff, raw[rows], NEG)
                s_ref[rows, c * TOK : (c + 1) * TOK] = s
                for g in range(3):
                    top[i] = jnp.maximum(top[i], s[:, g * BLOCK : (g + 1) * BLOCK])
        m = jnp.concatenate([jnp.max(t, axis=1, keepdims=True) for t in top], axis=0)
        total = jnp.zeros((TOK, BLOCK), F32)
        out = jnp.zeros((TOK, HD), F32)
        for c in range(WINDOW):
            p = jnp.exp2((s_ref[:, c * TOK : (c + 1) * TOK] - m) * (SCALE * LOG2E))
            for g in range(3):
                total = total + p[:, g * BLOCK : (g + 1) * BLOCK]
            pb = p.astype(BF)
            p_ref[:, c * TOK : (c + 1) * TOK] = pb
            out = out + dot_nt(pb, vt[:, win(c)])
        inv = 1.0 / jnp.sum(total, axis=1, keepdims=True)
        at_n = (out * inv).astype(BF).astype(F32)
        dos_n = (do_n * (inv * SCALE)).astype(BF)
        delta = jnp.sum(dos_n.astype(F32) * at_n, axis=1, keepdims=True)
        d_q = jnp.zeros((TOK, HD), F32)
        for c in range(WINDOW):
            cols = slice(c * TOK, (c + 1) * TOK)
            dp = dot_nn(dos_n, vt[:, win(c)])
            ds = (p_ref[:, cols].astype(F32) * (dp - delta)).astype(BF)
            ds_ref[:, cols] = ds
            d_q = d_q + dot_nt(ds, kt[:, win(c)])
        dos_t = dos_n.astype(F32).T.astype(BF)
        for c in range(WINDOW):
            cols = slice(c * TOK, (c + 1) * TOK)
            dk[:, win(c)] += dot_nn(qt[r], ds_ref[:, cols])
            dv[:, win(c)] += dot_nn(dos_t, p_ref[:, cols])
        attn_t = at_n.T.astype(BF)
        dq_t = d_q.T.astype(BF)
        both = jnp.concatenate([attn_t, dq_t], axis=0)
        early[:, pl.ds(at, TOK)] = both
        k_to = lax.rem(r - x + GROUP, GROUP)
        for k, out_k in enumerate((o0, o1, o2, o3)):
            @pl.when(k_to == k)
            def _():
                out_k[...] = both
        return carry

    lax.fori_loop(0, GROUP, step, 0)
    unscale = 1.0 / SCALE
    gp[:HD, :] = dk[:, :HALO].astype(BF)
    gp[HD:, :] = (dv[:, :HALO] * unscale).astype(BF)
    gn[:HD, :] = dk[:, HALO + ROW :].astype(BF)
    gn[HD:, :] = (dv[:, HALO + ROW :] * unscale).astype(BF)
    own[:HD, :] = dk[:, HALO : HALO + ROW]
    own[HD:, :] = dv[:, HALO : HALO + ROW] * unscale


def attention(place, parts, grads, from_prev, from_next):
    chunk = ((2 * HD, TOK), BF)
    outs = [((2 * HD, ROW), BF)] + [((2 * HD, HALO), BF)] * 2 + [((2 * HD, ROW), F32)] + [chunk] * 4
    scratch = [
        pltpu.VMEM((HD, KEYS), BF),
        pltpu.VMEM((HD, KEYS), BF),
        pltpu.VMEM((16, KEYS), F32),
        pltpu.VMEM((GROUP, 16, KEYS), F32),
        pltpu.VMEM((GROUP, HD, TOK), BF),
        pltpu.VMEM((GROUP, HD, TOK), BF),
        pltpu.VMEM((TOK, WINDOW * TOK), F32),
        pltpu.VMEM((TOK, WINDOW * TOK), BF),
        pltpu.VMEM((TOK, WINDOW * TOK), BF),
        pltpu.VMEM((HD, KEYS), F32),
        pltpu.VMEM((HD, KEYS), F32),
    ]
    return call(
        attention_kernel, outs, [place, *parts, *grads, from_prev, from_next], scratch,
        flops=12 * ROW * WINDOW * TOK * 128, moved=6_000_000, exps=ROW * WINDOW * TOK,
    )


def combine_kernel(place, own, from_next, from_prev, full, c0, c1, c2, c3):
    x = place[1]
    full[:, :TOK] = (own[:, :TOK] + from_prev[:, :TOK].astype(F32)).astype(BF)
    middle = own[:, TOK:HALO] + from_next[:, : HALO - TOK].astype(F32)
    full[:, TOK:HALO] = (middle + from_prev[:, TOK:].astype(F32)).astype(BF)
    full[:, HALO:] = (own[:, HALO:] + from_next[:, HALO - TOK :].astype(F32)).astype(BF)
    for k, out in enumerate((c0, c1, c2, c3)):
        at = pl.multiple_of(lax.rem(x + k, GROUP) * TOK, TOK)
        out[...] = full[:, pl.ds(at, TOK)]


def early_kernel(scale, values, tokens, cotangent, out):
    @pl.when(pl.program_id(0) == 0)
    def _():
        out[...] = jnp.zeros_like(out)

    out[:HD, :] += dot_nn(values[:HD, :], cotangent[...]) * scale
    out[HD:, :] += dot_nn(values[HD:, :], tokens[...]) * scale


def late_kernel(scale, place, early, values, tokens, send, keep, total):
    step = pl.program_id(0)

    @pl.when(step == 0)
    def _():
        total[...] = jnp.zeros_like(total)

    total[...] += dot_nn(values[...], tokens[...]) * scale

    @pl.when(step == pl.num_programs(0) - 1)
    def _():
        half = total.shape[1] // 2
        y = place[2]
        for other, out in ((1, send), (0, keep)):
            at = pl.multiple_of(lax.rem(y + other, 2) * half, half)
            cols = pl.ds(at, half)
            block = jnp.concatenate([early[:, cols], total[:, cols]], axis=0)
            out[...] = block.T.astype(out.dtype)


def token_block(width):
    return pl.BlockSpec((TOK, width), lambda i, *_: (i, 0))


def value_block():
    return pl.BlockSpec((2 * HD, TOK), lambda i, *_: (0, i))


def weights_early(scale, values, tokens, cotangent):
    model = tokens.shape[1]
    return pl.pallas_call(
        functools.partial(early_kernel, scale),
        grid=(GROUP,),
        in_specs=[value_block(), token_block(model), token_block(model)],
        out_specs=pl.BlockSpec((2 * HD, model), lambda i: (0, 0)),
        out_shape=jax.ShapeDtypeStruct((2 * HD, model), F32),
        compiler_params=pltpu.CompilerParams(vmem_limit_bytes=VMEM_LIMIT),
        cost_estimate=pl.CostEstimate(
            flops=4 * HD * ROW * model, bytes_accessed=8_000_000, transcendentals=0
        ),
    )(values, tokens, cotangent)


def weights_late(scale, place, early, values, tokens):
    model = tokens.shape[1]
    half = pl.BlockSpec((model // 2, 4 * HD), lambda i, place: (0, 0))
    return pl.pallas_call(
        functools.partial(late_kernel, scale),
        grid_spec=pltpu.PrefetchScalarGridSpec(
            num_scalar_prefetch=1,
            grid=(GROUP,),
            in_specs=[
                pl.BlockSpec((2 * HD, model), lambda i, place: (0, 0)),
                value_block(),
                token_block(model),
            ],
            out_specs=[half, half],
            scratch_shapes=[pltpu.VMEM((2 * HD, model), F32)],
        ),
        out_shape=[
            jax.ShapeDtypeStruct((model // 2, 4 * HD), BF),
            jax.ShapeDtypeStruct((model // 2, 4 * HD), F32),
        ],
        compiler_params=pltpu.CompilerParams(vmem_limit_bytes=VMEM_LIMIT),
        cost_estimate=pl.CostEstimate(
            flops=4 * HD * ROW * model, bytes_accessed=5_000_000, transcendentals=0
        ),
    )(place, early, values, tokens)


def share_kernel(pieces, place, *refs):
    count = GROUP * len(pieces)
    ins, (weights, send, keep, held) = refs[:count], refs[count:]
    x = place[1]
    core = place[3]
    for k in range(GROUP):
        head = lax.rem(x - k + GROUP, GROUP)
        done = 0
        for source, (first, parts) in enumerate(pieces):
            ref = ins[source * GROUP + k]
            for part in range(parts):
                row = first + part * HD
                held[done, head] = ref[row : row + HD, :]
                done += 1
    values = held[...].reshape(-1, held.shape[-1])
    local = GROUP * HD
    for other, out in ((1, send), (0, keep)):
        for h in range(2):
            at = pl.multiple_of((2 * h + lax.rem(core + other, 2)) * local, local)
            product = dot_nn(weights[pl.ds(at, local), :], values)
            out[h * local : (h + 1) * local, :] = product.astype(out.dtype)


def scatter_heads(place, pieces, values, weights):
    rows = weights.shape[0] // 2
    parts = weights.shape[1] // (GROUP * HD)
    send, keep = call(
        functools.partial(share_kernel, pieces),
        [((rows, TOK), BF), ((rows, TOK), F32)],
        [place, *values, weights],
        [pltpu.VMEM((parts, GROUP, HD, TOK), BF)],
        flops=4 * rows * weights.shape[1] * TOK, moved=4_000_000,
    )
    got = shift(send, "c", 1)
    half = (keep + got.astype(F32)).reshape(2, -1, TOK)
    h = lax.axis_index("h")
    other = lax.dynamic_index_in_dim(half, 1 - h, 0, keepdims=False).astype(BF)
    mine = lax.dynamic_index_in_dim(half, h, 0, keepdims=False)
    return (mine + shift(other, "h", 1).astype(F32)).astype(BF)


def on_device(tokens, w_qkv, w_out, cotangent, block_mask, regions):
    width, model = tokens.shape
    local = w_out.shape[0]
    x = lax.axis_index("x")
    y = lax.axis_index("y")
    row = y * (ROWS // 2) + lax.axis_index("z")
    place = jnp.stack([row, x, y, lax.axis_index("c")]).astype(jnp.int32)
    grad_scale = (width * lax.axis_size(SEQ_AXES)) ** (-0.5)
    w3 = w_qkv.transpose(1, 2, 0).reshape(3, GROUP, HD, model)

    *sent, tokens_part = call(
        project_kernel, [((256, width), BF)] * GROUP + [((width // 2, model), BF)],
        [place, w3, tokens, regions[None, :], block_mask],
        [pltpu.VMEM((16, width), F32), pltpu.VMEM((3, GROUP, HD, width), BF)],
        flops=2 * 3 * local * model * width, moved=5_000_000,
    )
    parts = [sent[0]] + [shift(sent[k], "x", k) for k in (1, 2, 3)]
    tokens_row = lax.all_gather(tokens_part, ("x", "c"), axis=0, tiled=True)
    *sent_grad, cot_part = call(
        project_grad_kernel, [((HD, width), BF)] * GROUP + [((width // 2, model), BF)],
        [place, w_out, cotangent],
        [pltpu.VMEM((GROUP, HD, width), BF)],
        flops=2 * local * model * width, moved=3_000_000,
    )
    grads = [sent_grad[0]] + [shift(sent_grad[k], "x", k) for k in (1, 2, 3)]
    cot_row = lax.all_gather(cot_part, ("x", "c"), axis=0, tiled=True)
    to_next, to_prev = call(
        halo_kernel, [((2 * HD + 16, HALO), BF)] * 2, [place, *parts], moved=2_000_000
    )
    from_prev = shift(to_next, ROW_AXES, 1)
    from_next = shift(to_prev, ROW_AXES, -1)
    w_late, _ = lax.optimization_barrier((w3, to_next))
    w_t, w_out_t = call(
        turn_kernel, [((model, 3 * local), BF), ((model, local), BF)],
        [place, w_late.reshape(3 * local, model), w_out], moved=6_000_000,
    )
    from_prev, from_next, w_t, w_out_t = lax.optimization_barrier(
        (from_prev, from_next, w_t, w_out_t)
    )

    early, gp, gn, own, *mine = attention(place, parts, grads, from_prev, from_next)
    back_next = shift(gp, ROW_AXES, -1)
    back_prev = shift(gn, ROW_AXES, 1)
    aq_all = [mine[0]] + [shift(mine[k], "x", k) for k in (1, 2, 3)]
    early_w = weights_early(grad_scale, early, tokens_row, cot_row)

    dkv, *kv_chunks = call(
        combine_kernel, [((2 * HD, ROW), BF)] + [((2 * HD, width), BF)] * GROUP,
        [place, own, back_next, back_prev], moved=3_000_000,
    )
    kv_all = [kv_chunks[0]] + [shift(kv_chunks[k], "x", k) for k in (1, 2, 3)]
    send_w, keep_w = weights_late(grad_scale, place, early_w, dkv, tokens_row)
    got_w = shift(send_w, "y", 1)
    mixed_t = scatter_heads(place, ((0, 1),), aq_all, w_out_t)
    grad_tokens_t = scatter_heads(place, ((HD, 1), (0, 2)), [*aq_all, *kv_all], w_t)

    half_w = (keep_w + got_w.astype(F32)).astype(BF).reshape(ROWS // 2, model // ROWS, 4 * HD)
    spread = lax.all_to_all(half_w, "z", 0, 0, tiled=True)
    summed = jnp.sum(spread.astype(F32), axis=0).reshape(GROUP, -1, 4 * HD)
    final = lax.all_to_all(summed, "x", 0, 0, tiled=True)
    share = final.shape[1]
    final = final.reshape(GROUP, share, 4, HD).transpose(1, 2, 0, 3).reshape(share, 4, local)
    return (mixed_t.T, grad_tokens_t.T, final[:, 1:], final[:, 0].T)


def solution(mesh):
    devices = mesh.devices.reshape(2, ROWS // 2, GROUP, 2, 2)
    fine = Mesh(devices, ("y", "z", "x", "h", "c"))
    placed = (
        P(SEQ_AXES, None),
        P(None, None, HEAD_AXES),
        P(HEAD_AXES, None),
        P(SEQ_AXES, None),
        P(SEQ_AXES, None),
        P(SEQ_AXES),
    )
    return jax.shard_map(
        on_device,
        mesh=fine,
        in_specs=placed,
        out_specs=(
            P(SEQ_AXES, HEAD_AXES),
            P(SEQ_AXES, HEAD_AXES),
            P(SEQ_AXES, None, HEAD_AXES),
            P(HEAD_AXES, SEQ_AXES),
        ),
        check_vma=False,
    )
```

```python
import functools

import jax
import jax.numpy as jnp
from jax import lax
from jax.experimental import pallas as pl
from jax.experimental.pallas import tpu as pltpu
from jax.sharding import Mesh
from jax.sharding import PartitionSpec as P

HD = 80
BLOCK = 128
SPAN = 3
TOK = 384
GROUP = 4
PIECES = GROUP + 2 * SPAN
WINDOW = 2 * SPAN + 1
ROW = GROUP * TOK
HALO = SPAN * TOK
KEYS = PIECES * TOK
ROWS = 16
NB = 192
SCALE = HD ** (-0.5)
LOG2E = 1.4426950408889634
NEG = -1e30
BF = jnp.bfloat16
F32 = jnp.float32
MIB = 1024 * 1024
SENT = 4 * HD + 16
ROW_AXES = ("y", "z")
SEQ_AXES = ("y", "z", "x")
HEAD_AXES = ("h", "c")


def shift(value, axis, steps):
    count = lax.axis_size(axis)
    return lax.ppermute(value, axis, [(i, (i + steps) % count) for i in range(count)])


def spec_vmem():
    return pl.BlockSpec(memory_space=pltpu.VMEM)


def spec_smem():
    return pl.BlockSpec(memory_space=pltpu.SMEM)


def call(kernel, outs, ins, scratch=(), mib=12, flops=0, moved=0, exps=0, spaces=None, out_spaces=None):
    anywhere = pl.BlockSpec(memory_space=pl.ANY)
    spec = {"v": spec_vmem(), "s": spec_smem(), "a": anywhere, "h": anywhere, "f": spec_vmem()}
    kept = {"h": pltpu.HBM, "f": pltpu.VMEM}
    spaces = spaces or "s" + "v" * (len(ins) - 1)
    out_spaces = out_spaces or "v" * len(outs)
    ins = [pltpu.with_memory_space_constraint(a, kept[c]) if c in kept else a for a, c in zip(ins, spaces)]
    return pl.pallas_call(
        kernel,
        out_shape=[kept.get(c, jax.ShapeDtypeStruct)(s, d) for (s, d), c in zip(outs, out_spaces)],
        in_specs=[spec[c] for c in spaces],
        out_specs=[spec[c] for c in out_spaces],
        scratch_shapes=list(scratch),
        compiler_params=pltpu.CompilerParams(vmem_limit_bytes=mib * MIB),
        cost_estimate=pl.CostEstimate(flops=flops, bytes_accessed=moved, transcendentals=exps),
    )(*ins)


def dot_nn(a, b):
    return lax.dot_general(a, b, (((1,), (0,)), ((), ())), preferred_element_type=F32)


def dot_nt(a, b):
    return lax.dot_general(a, b, (((1,), (1,)), ((), ())), preferred_element_type=F32)


def project_kernel(place, w, tokens, w_out, cotangent, regions, mask, o0, o1, o2, o3, parts,
                   wv, tv, wov, cv, rv, mv, extra, held, stage, sems):
    x = place[1]
    half = tokens.shape[0] // 2
    mine = pl.ds(pl.multiple_of(place[3] * half, half), half)
    pairs = ((w, wv), (tokens, tv), (w_out, wov), (cotangent, cv), (regions, rv), (mask, mv))
    copies = [pltpu.make_async_copy(a, b, sems.at[n]) for n, (a, b) in enumerate(pairs)]
    for n in (1, 0, 3, 2, 4, 5):
        copies[n].start()
    copies[4].wait()
    copies[5].wait()
    extra[...] = jnp.zeros_like(extra)
    extra[0:1, :] = rv[...].reshape(1, -1).astype(F32)
    extra[1:4, :NB] = mv[...].astype(F32)
    copies[1].wait()
    copies[0].wait()
    width = tokens.shape[0]
    held[:3] = dot_nt(wv[...], tv[...]).astype(BF).reshape(3, GROUP, HD, width)
    copies[3].wait()
    copies[2].wait()
    held[3] = dot_nt(wov[...], cv[...]).astype(BF).reshape(GROUP, HD, width)
    outs = []
    for k, out in enumerate((o0, o1, o2, o3)):
        head = lax.rem(x + k, GROUP)
        for piece in range(3):
            stage[k, piece * HD : (piece + 1) * HD, :] = held[piece, head]
        stage[k, 3 * HD : 3 * HD + 16, :] = extra[...].astype(BF)
        stage[k, 3 * HD + 16 :, :] = held[3, head]
        outs.append(pltpu.make_async_copy(stage.at[k], out, sems.at[6 + k]))
    outs.append(pltpu.make_async_copy(tv.at[mine], parts.at[0], sems.at[10]))
    outs.append(pltpu.make_async_copy(cv.at[mine], parts.at[1], sems.at[11]))
    for copy in outs:
        copy.start()
    for copy in outs:
        copy.wait()


def ready_kernel(place, r0, r1, r2, r3, w, w_out, wt, w_out_t, eff, qn, don):
    row = place[0]
    x = place[1]
    block_of = lax.broadcasted_iota(jnp.int32, (256, KEYS), 1) // BLOCK
    block_id = lax.rem(block_of + row * (ROW // BLOCK) - HALO // BLOCK + NB, NB)
    pick = jnp.where(block_id == lax.broadcasted_iota(jnp.int32, (256, KEYS), 0), 1.0, 0.0).astype(BF)
    for k, ref in enumerate((r0, r1, r2, r3)):
        pos = lax.rem(x - k + GROUP, GROUP)
        eff[pos] = dot_nn(ref[3 * HD : 3 * HD + 16, :256], pick)
        qn[pos] = ref[:HD, :].astype(F32).T.astype(BF)
        don[pos] = ref[3 * HD + 16 :, :].astype(F32).T
    wt[...] = w[...].T
    w_out_t[...] = w_out[...].T


def halo_kernel(place, r0, r1, r2, r3, to_next, to_prev):
    x = place[1]
    for k, ref in enumerate((r0, r1, r2, r3)):
        pos = lax.rem(x - k + GROUP, GROUP)

        @pl.when(pos >= 1)
        def _():
            at = pl.multiple_of((pos - 1) * TOK, TOK)
            to_next[:, pl.ds(at, TOK)] = ref[HD : 3 * HD + 16, :]

        @pl.when(pos <= 2)
        def _():
            at = pl.multiple_of(pos * TOK, TOK)
            to_prev[:, pl.ds(at, TOK)] = ref[HD : 3 * HD + 16, :]


def attention_kernel(place, r0, r1, r2, r3, eff, qn, don, from_prev, from_next,
                     early, gp, gn, own, o0, o1, o2, o3,
                     kt, vt, reg, qt, s_ref, p_ref, ds_ref, dk, dv):
    x = place[1]
    kt[:, :HALO] = from_prev[:HD, :]
    vt[:, :HALO] = from_prev[HD : 2 * HD, :]
    reg[:, :HALO] = from_prev[2 * HD :, :].astype(F32)
    kt[:, HALO + ROW :] = from_next[:HD, :]
    vt[:, HALO + ROW :] = from_next[HD : 2 * HD, :]
    reg[:, HALO + ROW :] = from_next[2 * HD :, :].astype(F32)
    for k, ref in enumerate((r0, r1, r2, r3)):
        pos = lax.rem(x - k + GROUP, GROUP)
        at = pl.multiple_of(HALO + pos * TOK, TOK)
        kt[:, pl.ds(at, TOK)] = ref[HD : 2 * HD, :]
        vt[:, pl.ds(at, TOK)] = ref[2 * HD : 3 * HD, :]
        reg[:, pl.ds(at, TOK)] = ref[3 * HD : 3 * HD + 16, :].astype(F32)
        qt[pos] = ref[:HD, :]
    dk[...] = jnp.zeros_like(dk)
    dv[...] = jnp.zeros_like(dv)

    def step(r, carry):
        at = pl.multiple_of(r * TOK, TOK)

        def win(c):
            return pl.ds(pl.multiple_of(at + c * TOK, TOK), TOK)

        q_n = qn[r]
        do_n = don[r]
        reg_q = reg[:, pl.ds(pl.multiple_of(HALO + at, TOK), TOK)].T[:, 0:1]
        top = [jnp.full((BLOCK, BLOCK), NEG, F32)] * 3
        for c in range(WINDOW):
            raw = dot_nn(q_n, kt[:, win(c)])
            key_reg = reg[0:1, win(c)]
            blocks = lax.broadcasted_iota(jnp.int32, (1, TOK), 1) // BLOCK
            for i in range(3):
                open_ = eff[r, 1 + i : 2 + i, win(c)] > 0.5
                if c == SPAN:
                    open_ = open_ | (blocks == i)
                key_eff = jnp.where(open_, key_reg, -1.0)
                rows = slice(i * BLOCK, (i + 1) * BLOCK)
                s = jnp.where(reg_q[rows] == key_eff, raw[rows], NEG)
                s_ref[rows, c * TOK : (c + 1) * TOK] = s
                for g in range(3):
                    top[i] = jnp.maximum(top[i], s[:, g * BLOCK : (g + 1) * BLOCK])
        m = jnp.concatenate([jnp.max(t, axis=1, keepdims=True) for t in top], axis=0)
        total = jnp.zeros((TOK, BLOCK), F32)
        out = jnp.zeros((TOK, HD), F32)
        for c in range(WINDOW):
            p = jnp.exp2((s_ref[:, c * TOK : (c + 1) * TOK] - m) * (SCALE * LOG2E))
            for g in range(3):
                total = total + p[:, g * BLOCK : (g + 1) * BLOCK]
            pb = p.astype(BF)
            p_ref[:, c * TOK : (c + 1) * TOK] = pb
            out = out + dot_nt(pb, vt[:, win(c)])
        inv = 1.0 / jnp.sum(total, axis=1, keepdims=True)
        at_n = (out * inv).astype(BF).astype(F32)
        dos_n = (do_n * (inv * SCALE)).astype(BF)
        delta = jnp.sum(dos_n.astype(F32) * at_n, axis=1, keepdims=True)
        d_q = jnp.zeros((TOK, HD), F32)
        for c in range(WINDOW):
            cols = slice(c * TOK, (c + 1) * TOK)
            dp = dot_nn(dos_n, vt[:, win(c)])
            ds = (p_ref[:, cols].astype(F32) * (dp - delta)).astype(BF)
            ds_ref[:, cols] = ds
            d_q = d_q + dot_nt(ds, kt[:, win(c)])
        dos_t = dos_n.astype(F32).T.astype(BF)
        for c in range(WINDOW):
            cols = slice(c * TOK, (c + 1) * TOK)
            dk[:, win(c)] += dot_nn(qt[r], ds_ref[:, cols])
            dv[:, win(c)] += dot_nn(dos_t, p_ref[:, cols])
        attn_t = at_n.T.astype(BF)
        dq_t = d_q.T.astype(BF)
        both = jnp.concatenate([attn_t, dq_t], axis=0)
        early[:, pl.ds(at, TOK)] = both
        k_to = lax.rem(r - x + GROUP, GROUP)
        for k, out_k in enumerate((o0, o1, o2, o3)):
            @pl.when(k_to == k)
            def _():
                out_k[...] = both
        return carry

    lax.fori_loop(0, GROUP, step, 0)
    unscale = 1.0 / SCALE
    gp[:HD, :] = dk[:, :HALO].astype(BF)
    gp[HD:, :] = (dv[:, :HALO] * unscale).astype(BF)
    gn[:HD, :] = dk[:, HALO + ROW :].astype(BF)
    gn[HD:, :] = (dv[:, HALO + ROW :] * unscale).astype(BF)
    own[:HD, :] = dk[:, HALO : HALO + ROW]
    own[HD:, :] = dv[:, HALO : HALO + ROW] * unscale


def attention(place, parts, ready, from_prev, from_next):
    chunk = ((2 * HD, TOK), BF)
    outs = [((2 * HD, ROW), BF)] + [((2 * HD, HALO), BF)] * 2 + [((2 * HD, ROW), F32)] + [chunk] * 4
    scratch = [
        pltpu.VMEM((HD, KEYS), BF),
        pltpu.VMEM((HD, KEYS), BF),
        pltpu.VMEM((16, KEYS), F32),
        pltpu.VMEM((GROUP, HD, TOK), BF),
        pltpu.VMEM((TOK, WINDOW * TOK), F32),
        pltpu.VMEM((TOK, WINDOW * TOK), BF),
        pltpu.VMEM((TOK, WINDOW * TOK), BF),
        pltpu.VMEM((HD, KEYS), F32),
        pltpu.VMEM((HD, KEYS), F32),
    ]
    return call(
        attention_kernel, outs, [place, *parts, *ready, from_prev, from_next], scratch, mib=28, out_spaces="f" * len(outs),
        flops=12 * ROW * WINDOW * TOK * 128, moved=6_000_000, exps=ROW * WINDOW * TOK,
    )


def combine_kernel(place, own, from_next, from_prev, full, c0, c1, c2, c3):
    x = place[1]
    full[:, :TOK] = (own[:, :TOK] + from_prev[:, :TOK].astype(F32)).astype(BF)
    middle = own[:, TOK:HALO] + from_next[:, : HALO - TOK].astype(F32)
    full[:, TOK:HALO] = (middle + from_prev[:, TOK:].astype(F32)).astype(BF)
    full[:, HALO:] = (own[:, HALO:] + from_next[:, HALO - TOK :].astype(F32)).astype(BF)
    for k, out in enumerate((c0, c1, c2, c3)):
        at = pl.multiple_of(lax.rem(x + k, GROUP) * TOK, TOK)
        out[...] = full[:, pl.ds(at, TOK)]


def early_kernel(scale, place, values, gathered, out, tokens, cotangent, sems):
    count, _, rows, _ = gathered.shape
    copies = []
    for which, into in ((1, cotangent), (0, tokens)):
        for n in range(count):
            sem = sems.at[which, n]
            copies.append(pltpu.make_async_copy(gathered.at[n, which], into.at[n * rows : (n + 1) * rows], sem))
    for copy in copies:
        copy.start()
    for copy in copies[:count]:
        copy.wait()
    out[:HD, :] = dot_nn(values[:HD, :], cotangent[...]) * scale
    for copy in copies[count:]:
        copy.wait()
    out[HD:, :] = dot_nn(values[HD:, :], tokens[...]) * scale


def late_kernel(scale, place, early, values, tokens, send, keep):
    half = early.shape[1] // 2
    y = place[2]
    for other, out in ((1, send), (0, keep)):
        cols = pl.ds(pl.multiple_of(lax.rem(y + other, 2) * half, half), half)
        out[: 2 * HD, :] = early[:, cols].astype(out.dtype)
        out[2 * HD :, :] = (dot_nn(values[...], tokens[:, cols]) * scale).astype(out.dtype)


def sum_turn_kernel(place, keep, got, out):
    out[...] = (keep[...] + got[...].astype(F32)).T.astype(BF)


def share_kernel(place, *refs):
    ins, (w_out_t, wt, send, keep, attn, grads) = refs[: 2 * GROUP], refs[2 * GROUP :]
    x = place[1]
    core = place[3]
    for k in range(GROUP):
        head = lax.rem(x - k + GROUP, GROUP)
        attn[head] = ins[k][:HD, :]
        grads[0, head] = ins[k][HD:, :]
        grads[1, head] = ins[GROUP + k][:HD, :]
        grads[2, head] = ins[GROUP + k][HD:, :]
    local = GROUP * HD
    for n, (weights, held) in enumerate(((w_out_t, attn), (wt, grads))):
        values = held[...].reshape(-1, TOK)
        for other, out in ((1, send), (0, keep)):
            for h in range(2):
                at = pl.multiple_of((2 * h + lax.rem(core + other, 2)) * local, local)
                out[n, h] = dot_nn(weights[pl.ds(at, local), :], values).astype(out.dtype)


def core_sum_kernel(place, keep, got, other, mine):
    h = place[4]
    for n in range(2):
        other[n] = (keep[n, 1 - h] + got[n, 1 - h].astype(F32)).astype(BF)
        mine[n] = keep[n, h] + got[n, h].astype(F32)


def head_sum_kernel(place, mine, got, mixed, grad):
    mixed[...] = (mine[0] + got[0].astype(F32)).astype(BF)
    grad[...] = (mine[1] + got[1].astype(F32)).astype(BF)


def scatter_core(place, values, w_out_t, wt):
    local = w_out_t.shape[1]
    model = w_out_t.shape[0]
    shape = (2, 2, local, TOK)
    send, keep = call(
        share_kernel,
        [(shape, BF), (shape, F32)],
        [place, *values, w_out_t, wt],
        [pltpu.VMEM((GROUP, HD, TOK), BF), pltpu.VMEM((3, GROUP, HD, TOK), BF)],
        mib=14, out_spaces="ff",
    )
    got = shift(send, "c", 1)
    return call(
        core_sum_kernel, [((2, local, TOK), BF), ((2, local, TOK), F32)], [place, keep, got],
        out_spaces="ff",
    )


def on_device(tokens, w_qkv, w_out, cotangent, block_mask, regions):
    width, model = tokens.shape
    local = w_out.shape[0]
    x = lax.axis_index("x")
    y = lax.axis_index("y")
    row = y * (ROWS // 2) + lax.axis_index("z")
    place = jnp.stack([row, x, y, lax.axis_index("c"), lax.axis_index("h")]).astype(jnp.int32)
    grad_scale = (width * lax.axis_size(SEQ_AXES)) ** (-0.5)
    w2 = w_qkv.transpose(1, 2, 0).reshape(3 * local, model)

    *sent, parts_mine = call(
        project_kernel,
        [((SENT, width), BF)] * GROUP + [((2, width // 2, model), BF)],
        [place, w2, tokens, w_out, cotangent, regions, block_mask],
        [
            pltpu.VMEM((3 * local, model), BF),
            pltpu.VMEM((width, model), BF),
            pltpu.VMEM((local, model), BF),
            pltpu.VMEM((width, model), BF),
            pltpu.VMEM(regions.shape, jnp.int32),
            pltpu.VMEM(block_mask.shape, jnp.int32),
            pltpu.VMEM((16, width), F32),
            pltpu.VMEM((4, GROUP, HD, width), BF),
            pltpu.VMEM((GROUP, SENT, width), BF),
            pltpu.SemaphoreType.DMA((12,)),
        ],
        mib=16, spaces="shhhhhh", out_spaces="hhhhh",
        flops=2 * 4 * local * model * width, moved=8_000_000,
    )
    parts = [sent[0]] + [shift(sent[k], "x", k) for k in (1, 2, 3)]
    gathered = lax.all_gather(parts_mine, ("x", "c"), axis=0)
    to_next, to_prev = call(
        halo_kernel, [((2 * HD + 16, HALO), BF)] * 2, [place, *parts], moved=2_000_000
    )
    from_prev = shift(to_next, ROW_AXES, 1)
    from_next = shift(to_prev, ROW_AXES, -1)
    w_late, _ = lax.optimization_barrier((w2, to_next))
    w_t, w_out_t, *ready = call(
        ready_kernel,
        [
            ((model, 3 * local), BF), ((model, local), BF),
            ((GROUP, 16, KEYS), F32), ((GROUP, width, HD), BF), ((GROUP, width, HD), F32),
        ],
        [place, *parts, w_late, w_out], moved=8_000_000, mib=20,
    )
    from_prev, from_next, ready = lax.optimization_barrier((from_prev, from_next, ready))

    early, gp, gn, own, *mine = attention(place, parts, ready, from_prev, from_next)
    back_next = shift(gp, ROW_AXES, -1)
    back_prev = shift(gn, ROW_AXES, 1)
    aq_all = [mine[0]] + [shift(mine[k], "x", k) for k in (1, 2, 3)]
    early_w, tokens_row = call(
        functools.partial(early_kernel, grad_scale),
        [((2 * HD, model), F32), ((ROW, model), BF)],
        [place, early, gathered],
        [pltpu.VMEM((ROW, model), BF), pltpu.SemaphoreType.DMA((2, 2 * GROUP))],
        spaces="svh", out_spaces="ff", mib=16,
    )
    back_next, back_prev, early_w = lax.optimization_barrier((back_next, back_prev, early_w))

    dkv, *kv_chunks = call(
        combine_kernel, [((2 * HD, ROW), BF)] + [((2 * HD, width), BF)] * GROUP,
        [place, own, back_next, back_prev], out_spaces="f" * 5,
    )
    kv_all = [kv_chunks[0]] + [shift(kv_chunks[k], "x", k) for k in (1, 2, 3)]
    send_w, keep_w = call(
        functools.partial(late_kernel, grad_scale),
        [((4 * HD, model // 2), BF), ((4 * HD, model // 2), F32)],
        [place, early_w, dkv, tokens_row], out_spaces="ff",
    )
    send_w, kv_all = lax.optimization_barrier((send_w, kv_all))
    got_w = shift(send_w, "y", 1)
    other, mine = scatter_core(place, [*aq_all, *kv_all], w_out_t, w_t)

    got_w, other = lax.optimization_barrier((got_w, other))
    got = shift(other, "h", 1)
    (half_w,) = call(
        sum_turn_kernel, [((model // 2, 4 * HD), BF)], [place, keep_w, got_w]
    )
    spread = lax.all_to_all(half_w.reshape(ROWS // 2, model // ROWS, 4 * HD), "z", 0, 0, tiled=True)
    summed = jnp.sum(spread.astype(F32), axis=0).reshape(GROUP, -1, 4 * HD)
    final = lax.all_to_all(summed, "x", 0, 0, tiled=True)
    mixed_t, grad_tokens_t = call(
        head_sum_kernel, [((local, width), BF)] * 2, [place, mine, got]
    )
    share = final.shape[1]
    final = final.reshape(GROUP, share, 4, HD).transpose(1, 2, 0, 3).reshape(share, 4, local)
    return (mixed_t.T, grad_tokens_t.T, final[:, 1:], final[:, 0].T)


def solution(mesh):
    devices = mesh.devices.reshape(2, ROWS // 2, GROUP, 2, 2)
    fine = Mesh(devices, ("y", "z", "x", "h", "c"))
    placed = (
        P(SEQ_AXES, None),
        P(None, None, HEAD_AXES),
        P(HEAD_AXES, None),
        P(SEQ_AXES, None),
        P(SEQ_AXES, None),
        P(SEQ_AXES),
    )
    return jax.shard_map(
        on_device,
        mesh=fine,
        in_specs=placed,
        out_specs=(
            P(SEQ_AXES, HEAD_AXES),
            P(SEQ_AXES, HEAD_AXES),
            P(SEQ_AXES, None, HEAD_AXES),
            P(HEAD_AXES, SEQ_AXES),
        ),
        check_vma=False,
    )
```

```python
import functools

import jax
import jax.numpy as jnp
from jax import lax
from jax.experimental import pallas as pl
from jax.experimental.pallas import tpu as pltpu
from jax.sharding import Mesh
from jax.sharding import PartitionSpec as P

HD = 80
BLOCK = 128
SPAN = 3
TOK = 384
GROUP = 4
PIECES = GROUP + 2 * SPAN
WINDOW = 2 * SPAN + 1
ROW = GROUP * TOK
HALO = SPAN * TOK
KEYS = PIECES * TOK
ROWS = 16
NB = 192
SCALE = HD ** (-0.5)
LOG2E = 1.4426950408889634
NEG = -1e30
BF = jnp.bfloat16
F32 = jnp.float32
MIB = 1024 * 1024
SENT = 4 * HD + 16
WIDE = ROW // 2
MAIN = 256
ROW_AXES = ("y", "z")
SEQ_AXES = ("y", "z", "x")
HEAD_AXES = ("h", "c")


def shift(value, axis, steps):
    count = lax.axis_size(axis)
    return lax.ppermute(value, axis, [(i, (i + steps) % count) for i in range(count)])


def spec_vmem():
    return pl.BlockSpec(memory_space=pltpu.VMEM)


def spec_smem():
    return pl.BlockSpec(memory_space=pltpu.SMEM)


def call(kernel, outs, ins, scratch=(), mib=12, flops=0, moved=0, exps=0, spaces=None, out_spaces=None):
    anywhere = pl.BlockSpec(memory_space=pl.ANY)
    spec = {"v": spec_vmem(), "s": spec_smem(), "a": anywhere, "h": anywhere, "f": spec_vmem()}
    kept = {"h": pltpu.HBM, "f": pltpu.VMEM}
    spaces = spaces or "s" + "v" * (len(ins) - 1)
    out_spaces = out_spaces or "v" * len(outs)
    ins = [pltpu.with_memory_space_constraint(a, kept[c]) if c in kept else a for a, c in zip(ins, spaces)]
    return pl.pallas_call(
        kernel,
        out_shape=[kept.get(c, jax.ShapeDtypeStruct)(s, d) for (s, d), c in zip(outs, out_spaces)],
        in_specs=[spec[c] for c in spaces],
        out_specs=[spec[c] for c in out_spaces],
        scratch_shapes=list(scratch),
        compiler_params=pltpu.CompilerParams(vmem_limit_bytes=mib * MIB),
        cost_estimate=pl.CostEstimate(flops=flops, bytes_accessed=moved, transcendentals=exps),
    )(*ins)


def dot_nn(a, b):
    return lax.dot_general(a, b, (((1,), (0,)), ((), ())), preferred_element_type=F32)


def dot_nt(a, b):
    return lax.dot_general(a, b, (((1,), (1,)), ((), ())), preferred_element_type=F32)


def project_kernel(place, w, tokens, w_out, cotangent, regions, mask, o0, o1, o2, o3, parts,
                   wv, tv, wov, cv, rv, mv, extra, held, stage, sems):
    x = place[1]
    half = tokens.shape[0] // 2
    mine = pl.ds(pl.multiple_of(place[3] * half, half), half)
    pairs = ((w, wv), (tokens, tv), (w_out, wov), (cotangent, cv), (regions, rv), (mask, mv))
    copies = [pltpu.make_async_copy(a, b, sems.at[n]) for n, (a, b) in enumerate(pairs)]
    for n in (1, 0, 3, 2, 4, 5):
        copies[n].start()
    copies[4].wait()
    copies[5].wait()
    extra[...] = jnp.zeros_like(extra)
    extra[0:1, :] = rv[...].reshape(1, -1).astype(F32)
    extra[1:4, :NB] = mv[...].astype(F32)
    copies[1].wait()
    copies[0].wait()
    width = tokens.shape[0]
    held[:3] = dot_nt(wv[...], tv[...]).astype(BF).reshape(3, GROUP, HD, width)
    copies[3].wait()
    copies[2].wait()
    held[3] = dot_nt(wov[...], cv[...]).astype(BF).reshape(GROUP, HD, width)
    outs = []
    for k, out in enumerate((o0, o1, o2, o3)):
        head = lax.rem(x + k, GROUP)
        into = out if k == 0 else stage.at[k]
        for piece in range(3):
            into[piece * HD : (piece + 1) * HD, :] = held[piece, head]
        into[3 * HD : 3 * HD + 16, :] = extra[...].astype(BF)
        into[3 * HD + 16 :, :] = held[3, head]
        if k > 0:
            outs.append(pltpu.make_async_copy(into, out, sems.at[6 + k]))
    outs.append(pltpu.make_async_copy(tv.at[mine], parts.at[0], sems.at[10]))
    outs.append(pltpu.make_async_copy(cv.at[mine], parts.at[1], sems.at[11]))
    for copy in outs:
        copy.start()
    for copy in outs:
        copy.wait()


def dot_tn(a, b):
    return lax.dot_general(a, b, (((0,), (0,)), ((), ())), preferred_element_type=F32)


def halo_kernel(place, r0, r1, r2, r3, to_next, to_prev):
    x = place[1]
    for k, ref in enumerate((r0, r1, r2, r3)):
        pos = lax.rem(x - k + GROUP, GROUP)

        @pl.when(pos >= 1)
        def _():
            at = pl.multiple_of((pos - 1) * TOK, TOK)
            to_next[:, pl.ds(at, TOK)] = ref[HD : 3 * HD + 16, :]

        @pl.when(pos <= 2)
        def _():
            at = pl.multiple_of(pos * TOK, TOK)
            to_prev[:, pl.ds(at, TOK)] = ref[HD : 3 * HD + 16, :]


def block_rows(i):
    return slice(i * BLOCK, (i + 1) * BLOCK)


def open_regions(eff, key_reg, first, i):
    opened = eff > 0.5
    if first is not None:
        blocks = lax.broadcasted_iota(jnp.int32, eff.shape, 1) // BLOCK
        opened = opened | (blocks == first + i)
    return jnp.where(opened, key_reg, -1.0)


def lane_sum(p):
    total = p[:, :BLOCK]
    for g in range(1, p.shape[1] // BLOCK):
        total = total + p[:, g * BLOCK : (g + 1) * BLOCK]
    return jnp.sum(total, axis=1, keepdims=True)


def lane_max(s):
    top = s[:, :BLOCK]
    for g in range(1, s.shape[1] // BLOCK):
        top = jnp.maximum(top, s[:, g * BLOCK : (g + 1) * BLOCK])
    return jnp.max(top, axis=1, keepdims=True)


def own_forward_kernel(place, r0, r1, r2, r3,
                       p1, m1, l1, o1, qn, don, qt, kt, vt, reg, eff_far,
                       eff_own, s_ref):
    row = place[0]
    x = place[1]
    lane = lax.broadcasted_iota(jnp.int32, (256, KEYS), 1) // BLOCK
    per_row = ROW // BLOCK
    per_halo = HALO // BLOCK
    ahead = jnp.where(lane < per_row, lane, jnp.where(lane < per_row + per_halo, lane - per_row - per_halo, lane - per_halo))
    block_id = lax.rem(ahead + row * per_row + NB, NB)
    pick = jnp.where(block_id == lax.broadcasted_iota(jnp.int32, (256, KEYS), 0), 1.0, 0.0).astype(BF)
    for k, ref in enumerate((r0, r1, r2, r3)):
        pos = lax.rem(x - k + GROUP, GROUP)
        cols = pl.ds(pl.multiple_of(pos * TOK, TOK), TOK)
        extra = ref[3 * HD : 3 * HD + 16, :]
        eff = dot_nn(extra[:, :256], pick)
        eff_own[pos] = eff[:, :ROW]
        eff_far[pos] = eff[:, ROW:]
        reg[:, cols] = extra.astype(F32)
        qt[:, cols] = ref[:HD, :]
        kt[:, cols] = ref[HD : 2 * HD, :]
        vt[:, cols] = ref[2 * HD : 3 * HD, :]
        qn[pos] = ref[:HD, :].astype(F32).T.astype(BF)
        don[pos] = ref[3 * HD + 16 :, :].astype(F32).T

    tops = []
    for r in range(GROUP):
        rows = slice(r * TOK, (r + 1) * TOK)
        reg_q = reg[:, rows].T[:, 0:1]
        raw = dot_nn(qn[r], kt[...])
        top = []
        for i in range(3):
            key_eff = open_regions(eff_own[r, 1 + i : 2 + i, :], reg[0:1, :], 3 * r, i)
            s = jnp.where(reg_q[block_rows(i)] == key_eff, raw[block_rows(i)], NEG)
            s_ref[r, block_rows(i), :] = s
            top.append(lane_max(s))
        tops.append(jnp.concatenate(top, axis=0))
        m1[r] = tops[r]
    for r in range(GROUP):
        rows = slice(r * TOK, (r + 1) * TOK)
        p = jnp.exp2((s_ref[r] - tops[r]) * (SCALE * LOG2E))
        p1[rows, :] = p.astype(BF)
        l1[r] = lane_sum(p)
        o1[r] = dot_nt(p1[rows, :], vt[...])


def far_kernel(place, eff_far, reg, qn, don, m1, l1, o1, qt, from_prev, from_next,
               gp, gn, attn, dos1, delta1, dq2,
               kh, vh, regh, s_ref, p_ref, ds_ref, dk, dv):
    for ref, cols in ((from_prev, slice(0, HALO)), (from_next, slice(HALO, 2 * HALO))):
        kh[:, cols] = ref[:HD, :]
        vh[:, cols] = ref[HD : 2 * HD, :]
        regh[:, cols] = ref[2 * HD :, :].astype(F32)
    dk[...] = jnp.zeros_like(dk)
    dv[...] = jnp.zeros_like(dv)

    tops = []
    for r in range(GROUP):
        rows = slice(r * TOK, (r + 1) * TOK)
        win = slice(r * TOK, r * TOK + HALO)
        reg_q = reg[:, rows].T[:, 0:1]
        raw = dot_nn(qn[r], kh[:, win])
        top = []
        for i in range(3):
            key_eff = open_regions(eff_far[r, 1 + i : 2 + i, win], regh[0:1, win], None, i)
            s = jnp.where(reg_q[block_rows(i)] == key_eff, raw[block_rows(i)], NEG)
            s_ref[r, block_rows(i), :] = s
            top.append(lane_max(s))
        tops.append(jnp.maximum(jnp.concatenate(top, axis=0), 0.1 * NEG))
    held = []
    for r in range(GROUP):
        win = slice(r * TOK, r * TOK + HALO)
        p = jnp.exp2((s_ref[r] - tops[r]) * (SCALE * LOG2E))
        p_ref[r] = p.astype(BF)
        held.append((lane_sum(p), dot_nt(p_ref[r], vh[:, win])))
    stats = []
    for r in range(GROUP):
        rows = slice(r * TOK, (r + 1) * TOK)
        m2 = tops[r]
        l2, o2 = held[r]
        m = jnp.maximum(m1[r], m2)
        w1 = jnp.exp2((m1[r] - m) * (SCALE * LOG2E))
        w2 = jnp.exp2((m2 - m) * (SCALE * LOG2E))
        inv = 1.0 / (l1[r] * w1 + l2 * w2)
        w1 = w1 * inv
        w2 = w2 * inv
        at_n = (o1[r] * w1 + o2 * w2).astype(BF).astype(F32)
        do_n = don[r]
        near = (do_n * (w1 * SCALE)).astype(BF)
        far = (do_n * (w2 * SCALE)).astype(BF)
        dos1[rows, :] = near
        delta1[r] = jnp.sum(near.astype(F32) * at_n, axis=1, keepdims=True)
        attn[:, rows] = at_n.T.astype(BF)
        stats.append((far, jnp.sum(far.astype(F32) * at_n, axis=1, keepdims=True)))
    for r in range(GROUP):
        rows = slice(r * TOK, (r + 1) * TOK)
        win = slice(r * TOK, r * TOK + HALO)
        far, delta2 = stats[r]
        dp = dot_nn(far, vh[:, win])
        ds_ref[r] = (p_ref[r].astype(F32) * (dp - delta2)).astype(BF)
        dq2[r] = dot_nt(ds_ref[r], kh[:, win])
    for r in range(GROUP):
        rows = slice(r * TOK, (r + 1) * TOK)
        win = slice(r * TOK, r * TOK + HALO)
        dk[:, win] += dot_nn(qt[:, rows], ds_ref[r])
        dv[:, win] += dot_nn(stats[r][0].astype(F32).T.astype(BF), p_ref[r])
    for out, cols in ((gp, slice(0, HALO)), (gn, slice(HALO, 2 * HALO))):
        out[:HD, :] = dk[:, cols].astype(BF)
        out[HD:, :] = (dv[:, cols] * (1.0 / SCALE)).astype(BF)


def own_backward_kernel(place, p1, dos1, delta1, dq2, qt, kt, vt, dq, own, ds_ref):
    def step(r, carry):
        rows = pl.ds(pl.multiple_of(r * TOK, TOK), TOK)
        d_q = dq2[r]
        near = dos1[rows, :]
        for c in range(2):
            cols = slice(c * WIDE, (c + 1) * WIDE)
            dp = dot_nn(near, vt[:, cols])
            ds = (p1[rows, cols].astype(F32) * (dp - delta1[r])).astype(BF)
            ds_ref[rows, cols] = ds
            d_q = d_q + dot_nt(ds, kt[:, cols])
        dq[:, rows] = d_q.T.astype(BF)
        return carry

    lax.fori_loop(0, GROUP, step, 0, unroll=True)
    dos_t = dos1[...].astype(F32).T.astype(BF)
    for c in range(2):
        cols = slice(c * WIDE, (c + 1) * WIDE)
        own[:HD, cols] = dot_nn(qt[...], ds_ref[:, cols])
        own[HD:, cols] = dot_nn(dos_t, p1[:, cols]) * (1.0 / SCALE)


def own_forward(place, parts):
    stat = ((GROUP, TOK, 1), F32)
    wide = ((GROUP, TOK, HD), F32)
    flat = ((HD, ROW), BF)
    outs = [((ROW, ROW), BF), stat, stat, wide, ((GROUP, TOK, HD), BF), wide, flat, flat, flat]
    outs = outs + [((16, ROW), F32), ((GROUP, 16, 2 * HALO), F32)]
    return call(
        own_forward_kernel, outs, [place, *parts],
        [pltpu.VMEM((GROUP, 16, ROW), F32), pltpu.VMEM((GROUP, TOK, ROW), F32)],
        mib=24, out_spaces="f" * len(outs),
        flops=4 * ROW * ROW * 128, moved=6_000_000, exps=ROW * ROW,
    )


def far_part(place, ins):
    outs = [((2 * HD, HALO), BF)] * 2 + [((HD, ROW), BF), ((ROW, HD), BF), ((GROUP, TOK, 1), F32)]
    outs = outs + [((GROUP, TOK, HD), F32)]
    scratch = [
        pltpu.VMEM((HD, 2 * HALO), BF),
        pltpu.VMEM((HD, 2 * HALO), BF),
        pltpu.VMEM((16, 2 * HALO), F32),
        pltpu.VMEM((GROUP, TOK, HALO), F32),
        pltpu.VMEM((GROUP, TOK, HALO), BF),
        pltpu.VMEM((GROUP, TOK, HALO), BF),
        pltpu.VMEM((HD, 2 * HALO), F32),
        pltpu.VMEM((HD, 2 * HALO), F32),
    ]
    return call(
        far_kernel, outs, [place, *ins], scratch, mib=28, out_spaces="f" * len(outs),
        flops=12 * ROW * HALO * 128, moved=6_000_000, exps=ROW * HALO,
    )


def own_backward(place, ins):
    return call(
        own_backward_kernel, [((HD, ROW), BF), ((2 * HD, ROW), F32)], [place, *ins],
        [pltpu.VMEM((ROW, ROW), BF)], mib=24, out_spaces="ff",
        flops=8 * ROW * ROW * 128, moved=6_000_000,
    )


def combine_kernel(place, attn, dq, own, from_next, from_prev, full, c0, c1, c2, c3):
    x = place[1]
    full[:HD, :] = attn[...]
    full[HD : 2 * HD, :] = dq[...]
    full[2 * HD :, :TOK] = (own[:, :TOK] + from_prev[:, :TOK].astype(F32)).astype(BF)
    middle = own[:, TOK:HALO] + from_next[:, : HALO - TOK].astype(F32)
    full[2 * HD :, TOK:HALO] = (middle + from_prev[:, TOK:].astype(F32)).astype(BF)
    full[2 * HD :, HALO:] = (own[:, HALO:] + from_next[:, HALO - TOK :].astype(F32)).astype(BF)
    for k, out in enumerate((c0, c1, c2, c3)):
        at = pl.multiple_of(lax.rem(x + k, GROUP) * TOK, TOK)
        out[...] = full[:, pl.ds(at, TOK)]


def weights_kernel(scale, place, values, gathered, out, tokens, cotangent, sems):
    parts, _, part_rows, _ = gathered.shape
    copies = []
    for which, into in ((0, tokens), (1, cotangent)):
        for n in range(parts):
            to = into.at[n * part_rows : (n + 1) * part_rows]
            copies.append(pltpu.make_async_copy(gathered.at[n, which], to, sems.at[which, n]))
    for copy in copies:
        copy.start()
    for copy in copies[:parts]:
        copy.wait()
    grads = dot_nn(values[HD:, :], tokens[...])
    for copy in copies[parts:]:
        copy.wait()
    total = (jnp.concatenate([dot_nn(values[:HD, :], cotangent[...]), grads], axis=0) * scale).T
    count = out.shape[0]
    rows = total.shape[0] // (2 * count)
    for z in range(count):
        first = total[z * rows : (z + 1) * rows]
        second = total[(count + z) * rows : (count + z + 1) * rows]
        both = jnp.concatenate([first, second], axis=0)
        out[z, : 2 * rows, :] = both[:, :MAIN].astype(BF)
        fold = rows // 2
        rest = [both[g * fold : (g + 1) * fold, MAIN:] for g in range(4)]
        folded = jnp.concatenate([jnp.concatenate(rest, axis=1), jnp.zeros((8, MAIN), F32)], axis=0)
        out[z, 2 * rows :, :] = folded.astype(BF)


def row_sum_kernel(place, spread, out):
    total = jnp.sum(spread[...].astype(F32), axis=0)
    count, share, _ = out.shape
    rest = count * share
    for n in range(count):
        at = rest + (n % 2) * share
        left = (n // 2) * (4 * HD - MAIN)
        out[n, :, :MAIN] = total[n * share : (n + 1) * share]
        out[n, :, MAIN:] = total[at : at + share, left : left + 4 * HD - MAIN]


def order_kernel(place, final, grad_qkv, grad_out):
    for h in range(GROUP):
        piece = final[h] + final[GROUP + h]
        cols = slice(h * HD, (h + 1) * HD)
        grad_out[:, cols] = piece[:, :HD]
        for part in range(3):
            grad_qkv[part, :, cols] = piece[:, (part + 1) * HD : (part + 2) * HD]


def share_kernel(place, *refs):
    ins, (w_out, w, send, keep, attn, grads, whole) = refs[:GROUP], refs[GROUP:]
    x = place[1]
    core = place[3]
    for k in range(GROUP):
        head = lax.rem(x - k + GROUP, GROUP)
        attn[head] = ins[k][:HD, :]
        for part in range(3):
            grads[part, head] = ins[k][(part + 1) * HD : (part + 2) * HD, :]
    local = GROUP * HD
    for n, (weights, held) in enumerate(((w_out, attn), (w, grads))):
        values = held[...].reshape(-1, TOK)
        whole[...] = dot_tn(weights[...], values)
        for other, out in ((1, send), (0, keep)):
            for h in range(2):
                at = pl.multiple_of((2 * h + lax.rem(core + other, 2)) * local, local)
                out[n, h] = whole[pl.ds(at, local), :].astype(out.dtype)


def core_sum_kernel(place, keep, got, other, mine):
    h = place[4]
    for n in range(2):
        other[n] = (keep[n, 1 - h] + got[n, 1 - h].astype(F32)).astype(BF)
        mine[n] = keep[n, h] + got[n, h].astype(F32)


def head_sum_kernel(place, mine, got, mixed, grad):
    mixed[...] = (mine[0] + got[0].astype(F32)).astype(BF)
    grad[...] = (mine[1] + got[1].astype(F32)).astype(BF)


def scatter_core(place, values, w_out, w):
    local, model = w_out.shape
    shape = (2, 2, local, TOK)
    send, keep = call(
        share_kernel,
        [(shape, BF), (shape, F32)],
        [place, *values, w_out, w],
        [
            pltpu.VMEM((GROUP, HD, TOK), BF),
            pltpu.VMEM((3, GROUP, HD, TOK), BF),
            pltpu.VMEM((model, TOK), F32),
        ],
        mib=16, out_spaces="ff",
    )
    got = shift(send, "c", 1)
    return call(
        core_sum_kernel, [((2, local, TOK), BF), ((2, local, TOK), F32)], [place, keep, got],
        out_spaces="ff",
    )


def on_device(tokens, w_qkv, w_out, cotangent, block_mask, regions):
    width, model = tokens.shape
    local = w_out.shape[0]
    x = lax.axis_index("x")
    y = lax.axis_index("y")
    row = y * (ROWS // 2) + lax.axis_index("z")
    place = jnp.stack([row, x, y, lax.axis_index("c"), lax.axis_index("h")]).astype(jnp.int32)
    grad_scale = (width * lax.axis_size(SEQ_AXES)) ** (-0.5)
    w2 = w_qkv.transpose(1, 2, 0).reshape(3 * local, model)

    *sent, parts_mine = call(
        project_kernel,
        [((SENT, width), BF)] * GROUP + [((2, width // 2, model), BF)],
        [place, w2, tokens, w_out, cotangent, regions, block_mask],
        [
            pltpu.VMEM((3 * local, model), BF),
            pltpu.VMEM((width, model), BF),
            pltpu.VMEM((local, model), BF),
            pltpu.VMEM((width, model), BF),
            pltpu.VMEM(regions.shape, jnp.int32),
            pltpu.VMEM(block_mask.shape, jnp.int32),
            pltpu.VMEM((16, width), F32),
            pltpu.VMEM((4, GROUP, HD, width), BF),
            pltpu.VMEM((GROUP, SENT, width), BF),
            pltpu.SemaphoreType.DMA((12,)),
        ],
        mib=16, spaces="shhhhhh", out_spaces="fhhhh",
        flops=2 * 4 * local * model * width, moved=8_000_000,
    )
    parts = [sent[0]] + [shift(sent[k], "x", k) for k in (1, 2, 3)]
    gathered = lax.all_gather(parts_mine, ("x", "c"), axis=0)
    to_next, to_prev = call(
        halo_kernel, [((2 * HD + 16, HALO), BF)] * 2, [place, *parts], moved=2_000_000
    )
    from_prev = shift(to_next, ROW_AXES, 1)
    from_next = shift(to_prev, ROW_AXES, -1)
    held = own_forward(place, parts)
    p1, m1, l1, o1, qn, don, qt, kt, vt, reg, eff_far = held

    gp, gn, attn, dos1, delta1, dq2 = far_part(
        place, [eff_far, reg, qn, don, m1, l1, o1, qt, from_prev, from_next]
    )
    back_next = shift(gp, ROW_AXES, -1)
    back_prev = shift(gn, ROW_AXES, 1)
    dq, own = own_backward(place, [p1, dos1, delta1, dq2, qt, kt, vt])
    d_all, *chunks = call(
        combine_kernel, [((4 * HD, ROW), BF)] + [((4 * HD, width), BF)] * GROUP,
        [place, attn, dq, own, back_next, back_prev], out_spaces="f" * 5,
    )
    kv_all = [chunks[0]] + [shift(chunks[k], "x", k) for k in (1, 2, 3)]
    share = model // ROWS // GROUP
    gathered, d_all = lax.optimization_barrier((gathered, d_all))
    (terms,) = call(
        functools.partial(weights_kernel, grad_scale),
        [((ROWS // 2, 8 * share + 48, MAIN), BF)],
        [place, d_all, gathered],
        [
            pltpu.VMEM((ROW, model), BF),
            pltpu.VMEM((ROW, model), BF),
            pltpu.SemaphoreType.DMA((2, 2 * GROUP)),
        ],
        spaces="svh", out_spaces="f", mib=20,
    )
    spread = lax.all_to_all(terms, "z", 0, 0, tiled=True)
    other, mine = scatter_core(place, kv_all, w_out, w2)
    got = shift(other, "h", 1)
    (summed,) = call(row_sum_kernel, [((2 * GROUP, share, 4 * HD), F32)], [place, spread], out_spaces="f")
    final = lax.all_to_all(summed, ("y", "x"), 0, 0, tiled=True)
    mixed_t, grad_tokens_t = call(head_sum_kernel, [((local, width), BF)] * 2, [place, mine, got])
    final, mixed_t = lax.optimization_barrier((final, mixed_t))
    grad_qkv_t, grad_out_t = call(
        order_kernel, [((3, share, local), F32), ((share, local), F32)], [place, final]
    )
    return (mixed_t.T, grad_tokens_t.T, grad_qkv_t.transpose(1, 0, 2), grad_out_t.T)


def solution(mesh):
    devices = mesh.devices.reshape(2, ROWS // 2, GROUP, 2, 2)
    fine = Mesh(devices, ("y", "z", "x", "h", "c"))
    placed = (
        P(SEQ_AXES, None),
        P(None, None, HEAD_AXES),
        P(HEAD_AXES, None),
        P(SEQ_AXES, None),
        P(SEQ_AXES, None),
        P(SEQ_AXES),
    )
    return jax.shard_map(
        on_device,
        mesh=fine,
        in_specs=placed,
        out_specs=(
            P(SEQ_AXES, HEAD_AXES),
            P(SEQ_AXES, HEAD_AXES),
            P(SEQ_AXES, None, HEAD_AXES),
            P(HEAD_AXES, SEQ_AXES),
        ),
        check_vma=False,
    )
```

```python
import functools

import jax
import jax.numpy as jnp
from jax import lax
from jax.experimental import pallas as pl
from jax.experimental.pallas import tpu as pltpu
from jax.sharding import Mesh
from jax.sharding import PartitionSpec as P

HD = 80
BLOCK = 128
SPAN = 3
TOK = 384
GROUP = 4
PIECES = GROUP + 2 * SPAN
WINDOW = 2 * SPAN + 1
ROW = GROUP * TOK
HALO = SPAN * TOK
KEYS = PIECES * TOK
ROWS = 16
NB = 192
SCALE = HD ** (-0.5)
LOG2E = 1.4426950408889634
NEG = -1e30
BF = jnp.bfloat16
F32 = jnp.float32
MIB = 1024 * 1024
SENT = 3 * HD + 16
WIDE = ROW // 2
MAIN = 256
ROW_AXES = ("y", "z")
SEQ_AXES = ("y", "z", "x")
HEAD_AXES = ("h", "c")


def shift(value, axis, steps):
    count = lax.axis_size(axis)
    return lax.ppermute(value, axis, [(i, (i + steps) % count) for i in range(count)])


def spec_vmem():
    return pl.BlockSpec(memory_space=pltpu.VMEM)


def spec_smem():
    return pl.BlockSpec(memory_space=pltpu.SMEM)


def call(kernel, outs, ins, scratch=(), mib=12, flops=0, moved=0, exps=0, spaces=None, out_spaces=None):
    anywhere = pl.BlockSpec(memory_space=pl.ANY)
    spec = {"v": spec_vmem(), "s": spec_smem(), "a": anywhere, "h": anywhere, "f": spec_vmem()}
    kept = {"h": pltpu.HBM, "f": pltpu.VMEM}
    spaces = spaces or "s" + "v" * (len(ins) - 1)
    out_spaces = out_spaces or "v" * len(outs)
    ins = [pltpu.with_memory_space_constraint(a, kept[c]) if c in kept else a for a, c in zip(ins, spaces)]
    return pl.pallas_call(
        kernel,
        out_shape=[kept.get(c, jax.ShapeDtypeStruct)(s, d) for (s, d), c in zip(outs, out_spaces)],
        in_specs=[spec[c] for c in spaces],
        out_specs=[spec[c] for c in out_spaces],
        scratch_shapes=list(scratch),
        compiler_params=pltpu.CompilerParams(vmem_limit_bytes=mib * MIB),
        cost_estimate=pl.CostEstimate(flops=flops, bytes_accessed=moved, transcendentals=exps),
    )(*ins)


def dot_nn(a, b):
    return lax.dot_general(a, b, (((1,), (0,)), ((), ())), preferred_element_type=F32)


def dot_nt(a, b):
    return lax.dot_general(a, b, (((1,), (1,)), ((), ())), preferred_element_type=F32)


def halves_kernel(place, tokens, cotangent, parts, held, sems):
    half = tokens.shape[0] // 2
    mine = pl.ds(pl.multiple_of(place[3] * half, half), half)
    loads = [pltpu.make_async_copy(a.at[mine], held.at[n], sems.at[n]) for n, a in enumerate((tokens, cotangent))]
    stores = [pltpu.make_async_copy(held.at[n], parts.at[n], sems.at[2 + n]) for n in range(2)]
    for copy in loads:
        copy.start()
    for load, store in zip(loads, stores):
        load.wait()
        store.start()
    for copy in stores:
        copy.wait()


def project_kernel(place, w, tokens, regions, mask, o0, o1, o2, o3, wv, tv, rv, mv, extra, held, stage, sems):
    x = place[1]
    width = tokens.shape[0]
    local = GROUP * HD
    pairs = [(tokens, tv)] + [(w.at[n * local : (n + 1) * local], wv.at[n]) for n in range(3)]
    pairs = pairs + [(regions, rv), (mask, mv)]
    copies = [pltpu.make_async_copy(a, b, sems.at[n]) for n, (a, b) in enumerate(pairs)]
    for copy in copies:
        copy.start()
    outs = []
    copies[0].wait()
    for n in range(3):
        copies[1 + n].wait()
        held[n] = dot_nt(wv[n], tv[...]).astype(BF).reshape(GROUP, HD, width)
    copies[4].wait()
    copies[5].wait()
    extra[...] = jnp.zeros_like(extra)
    extra[0:1, :] = rv[...].reshape(1, -1).astype(F32)
    extra[1:4, :NB] = mv[...].astype(F32)
    for k, out in enumerate((o0, o1, o2, o3)):
        head = lax.rem(x + k, GROUP)
        into = out if k == 0 else stage.at[k]
        for piece in range(3):
            into[piece * HD : (piece + 1) * HD, :] = held[piece, head]
        into[3 * HD :, :] = extra[...].astype(BF)
        if k > 0:
            copy = pltpu.make_async_copy(into, out, sems.at[8 + k])
            copy.start()
            outs.append(copy)
    for copy in outs:
        copy.wait()


def project_grad_kernel(place, w_out, cotangent, o0, o1, o2, o3, held):
    x = place[1]
    held[...] = dot_nt(w_out[...], cotangent[...]).astype(BF).reshape(GROUP, HD, -1)
    for k, out in enumerate((o0, o1, o2, o3)):
        out[...] = held[lax.rem(x + k, GROUP)]


def dot_tn(a, b):
    return lax.dot_general(a, b, (((0,), (0,)), ((), ())), preferred_element_type=F32)


def halo_kernel(place, r0, r1, r2, r3, to_next, to_prev):
    x = place[1]
    for k, ref in enumerate((r0, r1, r2, r3)):
        pos = lax.rem(x - k + GROUP, GROUP)

        @pl.when(pos >= 1)
        def _():
            at = pl.multiple_of((pos - 1) * TOK, TOK)
            to_next[:, pl.ds(at, TOK)] = ref[HD : 3 * HD + 16, :]

        @pl.when(pos <= 2)
        def _():
            at = pl.multiple_of(pos * TOK, TOK)
            to_prev[:, pl.ds(at, TOK)] = ref[HD : 3 * HD + 16, :]


def block_rows(i):
    return slice(i * BLOCK, (i + 1) * BLOCK)


def open_regions(eff, key_reg, first, i):
    opened = eff > 0.5
    if first is not None:
        blocks = lax.broadcasted_iota(jnp.int32, eff.shape, 1) // BLOCK
        opened = opened | (blocks == first + i)
    return jnp.where(opened, key_reg, -1.0)


def lane_sum(p):
    total = p[:, :BLOCK]
    for g in range(1, p.shape[1] // BLOCK):
        total = total + p[:, g * BLOCK : (g + 1) * BLOCK]
    return jnp.sum(total, axis=1, keepdims=True)


def lane_max(s):
    top = s[:, :BLOCK]
    for g in range(1, s.shape[1] // BLOCK):
        top = jnp.maximum(top, s[:, g * BLOCK : (g + 1) * BLOCK])
    return jnp.max(top, axis=1, keepdims=True)


def own_forward_kernel(place, r0, r1, r2, r3,
                       p1, m1, l1, o1, qn, qt, kt, vt, reg, eff_far,
                       eff_own, s_ref):
    row = place[0]
    x = place[1]
    lane = lax.broadcasted_iota(jnp.int32, (256, KEYS), 1) // BLOCK
    per_row = ROW // BLOCK
    per_halo = HALO // BLOCK
    ahead = jnp.where(lane < per_row, lane, jnp.where(lane < per_row + per_halo, lane - per_row - per_halo, lane - per_halo))
    block_id = lax.rem(ahead + row * per_row + NB, NB)
    pick = jnp.where(block_id == lax.broadcasted_iota(jnp.int32, (256, KEYS), 0), 1.0, 0.0).astype(BF)
    for k, ref in enumerate((r0, r1, r2, r3)):
        pos = lax.rem(x - k + GROUP, GROUP)
        cols = pl.ds(pl.multiple_of(pos * TOK, TOK), TOK)
        extra = ref[3 * HD : 3 * HD + 16, :]
        eff = dot_nn(extra[:, :256], pick)
        eff_own[pos] = eff[:, :ROW]
        eff_far[pos] = eff[:, ROW:]
        reg[:, cols] = extra.astype(F32)
        qt[:, cols] = ref[:HD, :]
        kt[:, cols] = ref[HD : 2 * HD, :]
        vt[:, cols] = ref[2 * HD : 3 * HD, :]
        qn[pos] = ref[:HD, :].astype(F32).T.astype(BF)

    tops = []
    for r in range(GROUP):
        rows = slice(r * TOK, (r + 1) * TOK)
        reg_q = reg[:, rows].T[:, 0:1]
        raw = dot_nn(qn[r], kt[...])
        top = []
        for i in range(3):
            key_eff = open_regions(eff_own[r, 1 + i : 2 + i, :], reg[0:1, :], 3 * r, i)
            s = jnp.where(reg_q[block_rows(i)] == key_eff, raw[block_rows(i)], NEG)
            s_ref[r, block_rows(i), :] = s
            top.append(lane_max(s))
        tops.append(jnp.concatenate(top, axis=0))
        m1[r] = tops[r]
    for r in range(GROUP):
        rows = slice(r * TOK, (r + 1) * TOK)
        p = jnp.exp2((s_ref[r] - tops[r]) * (SCALE * LOG2E))
        p1[rows, :] = p.astype(BF)
        l1[r] = lane_sum(p)
        o1[r] = dot_nt(p1[rows, :], vt[...])


def far_kernel(place, d0, d1, d2, d3, eff_far, reg, qn, m1, l1, o1, qt, from_prev, from_next,
               gp, gn, attn, dos1, delta1, dq2,
               kh, vh, regh, s_ref, p_ref, ds_ref, dk, dv, don):
    x = place[1]
    for k, ref in enumerate((d0, d1, d2, d3)):
        don[lax.rem(x - k + GROUP, GROUP)] = ref[...].astype(F32).T
    for ref, cols in ((from_prev, slice(0, HALO)), (from_next, slice(HALO, 2 * HALO))):
        kh[:, cols] = ref[:HD, :]
        vh[:, cols] = ref[HD : 2 * HD, :]
        regh[:, cols] = ref[2 * HD :, :].astype(F32)
    dk[...] = jnp.zeros_like(dk)
    dv[...] = jnp.zeros_like(dv)

    tops = []
    for r in range(GROUP):
        rows = slice(r * TOK, (r + 1) * TOK)
        win = slice(r * TOK, r * TOK + HALO)
        reg_q = reg[:, rows].T[:, 0:1]
        raw = dot_nn(qn[r], kh[:, win])
        top = []
        for i in range(3):
            key_eff = open_regions(eff_far[r, 1 + i : 2 + i, win], regh[0:1, win], None, i)
            s = jnp.where(reg_q[block_rows(i)] == key_eff, raw[block_rows(i)], NEG)
            s_ref[r, block_rows(i), :] = s
            top.append(lane_max(s))
        tops.append(jnp.maximum(jnp.concatenate(top, axis=0), 0.1 * NEG))
    held = []
    for r in range(GROUP):
        win = slice(r * TOK, r * TOK + HALO)
        p = jnp.exp2((s_ref[r] - tops[r]) * (SCALE * LOG2E))
        p_ref[r] = p.astype(BF)
        held.append((lane_sum(p), dot_nt(p_ref[r], vh[:, win])))
    stats = []
    for r in range(GROUP):
        rows = slice(r * TOK, (r + 1) * TOK)
        m2 = tops[r]
        l2, o2 = held[r]
        m = jnp.maximum(m1[r], m2)
        w1 = jnp.exp2((m1[r] - m) * (SCALE * LOG2E))
        w2 = jnp.exp2((m2 - m) * (SCALE * LOG2E))
        inv = 1.0 / (l1[r] * w1 + l2 * w2)
        w1 = w1 * inv
        w2 = w2 * inv
        at_n = (o1[r] * w1 + o2 * w2).astype(BF).astype(F32)
        do_n = don[r]
        near = (do_n * (w1 * SCALE)).astype(BF)
        far = (do_n * (w2 * SCALE)).astype(BF)
        dos1[rows, :] = near
        delta1[r] = jnp.sum(near.astype(F32) * at_n, axis=1, keepdims=True)
        attn[:, rows] = at_n.T.astype(BF)
        stats.append((far, jnp.sum(far.astype(F32) * at_n, axis=1, keepdims=True)))
    for r in range(GROUP):
        rows = slice(r * TOK, (r + 1) * TOK)
        win = slice(r * TOK, r * TOK + HALO)
        far, delta2 = stats[r]
        dp = dot_nn(far, vh[:, win])
        ds_ref[r] = (p_ref[r].astype(F32) * (dp - delta2)).astype(BF)
        dq2[r] = dot_nt(ds_ref[r], kh[:, win])
    for r in range(GROUP):
        rows = slice(r * TOK, (r + 1) * TOK)
        win = slice(r * TOK, r * TOK + HALO)
        dk[:, win] += dot_nn(qt[:, rows], ds_ref[r])
        dv[:, win] += dot_nn(stats[r][0].astype(F32).T.astype(BF), p_ref[r])
    for out, cols in ((gp, slice(0, HALO)), (gn, slice(HALO, 2 * HALO))):
        out[:HD, :] = dk[:, cols].astype(BF)
        out[HD:, :] = (dv[:, cols] * (1.0 / SCALE)).astype(BF)


def own_backward_kernel(place, p1, dos1, delta1, dq2, qt, kt, vt, dq, own, ds_ref):
    def step(r, carry):
        rows = pl.ds(pl.multiple_of(r * TOK, TOK), TOK)
        d_q = dq2[r]
        near = dos1[rows, :]
        for c in range(2):
            cols = slice(c * WIDE, (c + 1) * WIDE)
            dp = dot_nn(near, vt[:, cols])
            ds = (p1[rows, cols].astype(F32) * (dp - delta1[r])).astype(BF)
            ds_ref[rows, cols] = ds
            d_q = d_q + dot_nt(ds, kt[:, cols])
        dq[:, rows] = d_q.T.astype(BF)
        return carry

    lax.fori_loop(0, GROUP, step, 0, unroll=True)
    dos_t = dos1[...].astype(F32).T.astype(BF)
    for c in range(2):
        cols = slice(c * WIDE, (c + 1) * WIDE)
        own[:HD, cols] = dot_nn(qt[...], ds_ref[:, cols])
        own[HD:, cols] = dot_nn(dos_t, p1[:, cols]) * (1.0 / SCALE)


def own_forward(place, parts):
    stat = ((GROUP, TOK, 1), F32)
    wide = ((GROUP, TOK, HD), F32)
    flat = ((HD, ROW), BF)
    outs = [((ROW, ROW), BF), stat, stat, wide, ((GROUP, TOK, HD), BF), flat, flat, flat]
    outs = outs + [((16, ROW), F32), ((GROUP, 16, 2 * HALO), F32)]
    return call(
        own_forward_kernel, outs, [place, *parts],
        [pltpu.VMEM((GROUP, 16, ROW), F32), pltpu.VMEM((GROUP, TOK, ROW), F32)],
        mib=24, out_spaces="f" * len(outs),
        flops=4 * ROW * ROW * 128, moved=6_000_000, exps=ROW * ROW,
    )


def far_part(place, ins):
    outs = [((2 * HD, HALO), BF)] * 2 + [((HD, ROW), BF), ((ROW, HD), BF), ((GROUP, TOK, 1), F32)]
    outs = outs + [((GROUP, TOK, HD), F32)]
    scratch = [
        pltpu.VMEM((HD, 2 * HALO), BF),
        pltpu.VMEM((HD, 2 * HALO), BF),
        pltpu.VMEM((16, 2 * HALO), F32),
        pltpu.VMEM((GROUP, TOK, HALO), F32),
        pltpu.VMEM((GROUP, TOK, HALO), BF),
        pltpu.VMEM((GROUP, TOK, HALO), BF),
        pltpu.VMEM((HD, 2 * HALO), F32),
        pltpu.VMEM((HD, 2 * HALO), F32),
        pltpu.VMEM((GROUP, TOK, HD), F32),
    ]
    return call(
        far_kernel, outs, [place, *ins], scratch, mib=28, out_spaces="f" * len(outs),
        flops=12 * ROW * HALO * 128, moved=6_000_000, exps=ROW * HALO,
    )


def own_backward(place, ins):
    return call(
        own_backward_kernel, [((HD, ROW), BF), ((2 * HD, ROW), F32)], [place, *ins],
        [pltpu.VMEM((ROW, ROW), BF)], mib=24, out_spaces="ff",
        flops=8 * ROW * ROW * 128, moved=6_000_000,
    )


def combine_kernel(place, attn, dq, own, from_next, from_prev, full, c0, c1, c2, c3, stage, sem):
    x = place[1]
    full[:HD, :] = attn[...]
    full[HD : 2 * HD, :] = dq[...]
    full[2 * HD :, :TOK] = (own[:, :TOK] + from_prev[:, :TOK].astype(F32)).astype(BF)
    middle = own[:, TOK:HALO] + from_next[:, : HALO - TOK].astype(F32)
    full[2 * HD :, TOK:HALO] = (middle + from_prev[:, TOK:].astype(F32)).astype(BF)
    full[2 * HD :, HALO:] = (own[:, HALO:] + from_next[:, HALO - TOK :].astype(F32)).astype(BF)
    for k, out in enumerate((stage, c1, c2, c3)):
        at = pl.multiple_of(lax.rem(x + k, GROUP) * TOK, TOK)
        out[...] = full[:, pl.ds(at, TOK)]
        if k == 0:
            copy = pltpu.make_async_copy(stage, c0, sem)
            copy.start()
    copy.wait()


def weights_kernel(scale, place, values, gathered, out, tokens, cotangent, sems):
    parts, _, part_rows, _ = gathered.shape
    copies = []
    for which, into in ((1, cotangent), (0, tokens)):
        for n in range(parts):
            to = into.at[n * part_rows : (n + 1) * part_rows]
            copies.append(pltpu.make_async_copy(gathered.at[n, which], to, sems.at[which, n]))
    for copy in copies:
        copy.start()
    for copy in copies[:parts]:
        copy.wait()
    first = dot_nn(values[:HD, :], cotangent[...])
    for copy in copies[parts:]:
        copy.wait()
    total = (jnp.concatenate([first, dot_nn(values[HD:, :], tokens[...])], axis=0) * scale).T
    count = out.shape[0]
    rows = total.shape[0] // (2 * count)
    for z in range(count):
        first = total[z * rows : (z + 1) * rows]
        second = total[(count + z) * rows : (count + z + 1) * rows]
        both = jnp.concatenate([first, second], axis=0)
        out[z, : 2 * rows, :] = both[:, :MAIN].astype(BF)
        fold = rows // 2
        rest = [both[g * fold : (g + 1) * fold, MAIN:] for g in range(4)]
        folded = jnp.concatenate([jnp.concatenate(rest, axis=1), jnp.zeros((8, MAIN), F32)], axis=0)
        out[z, 2 * rows :, :] = folded.astype(BF)


def row_sum_kernel(place, spread, out):
    total = jnp.sum(spread[...].astype(F32), axis=0)
    count, share, _ = out.shape
    rest = count * share
    for n in range(count):
        at = rest + (n % 2) * share
        left = (n // 2) * (4 * HD - MAIN)
        out[n, :, :MAIN] = total[n * share : (n + 1) * share]
        out[n, :, MAIN:] = total[at : at + share, left : left + 4 * HD - MAIN]


def order_kernel(place, final, grad_qkv, grad_out):
    for h in range(GROUP):
        piece = final[h] + final[GROUP + h]
        cols = slice(h * HD, (h + 1) * HD)
        grad_out[:, cols] = piece[:, :HD]
        for part in range(3):
            grad_qkv[part, :, cols] = piece[:, (part + 1) * HD : (part + 2) * HD]


def share_kernel(place, mine, r1, r2, r3, w_out, w, send, keep, attn, grads, whole, mv, wov, wv, sems):
    pairs = ((mine, mv), (w_out, wov), (w, wv))
    copies = [pltpu.make_async_copy(a, b, sems.at[n]) for n, (a, b) in enumerate(pairs)]
    for copy in copies:
        copy.start()
    x = place[1]
    core = place[3]
    for k, ref in enumerate((r1, r2, r3, mv)):
        if ref is mv:
            copies[0].wait()
        head = lax.rem(x - (k + 1) + GROUP, GROUP)
        attn[head] = ref[:HD, :]
        for part in range(3):
            grads[part, head] = ref[(part + 1) * HD : (part + 2) * HD, :]
    local = GROUP * HD
    for n, (weights, held) in enumerate(((wov, attn), (wv, grads))):
        copies[n + 1].wait()
        values = held[...].reshape(-1, TOK)
        whole[...] = dot_tn(weights[...], values)
        for other, out in ((1, send), (0, keep)):
            for h in range(2):
                at = pl.multiple_of((2 * h + lax.rem(core + other, 2)) * local, local)
                out[n, h] = whole[pl.ds(at, local), :].astype(out.dtype)


def core_sum_kernel(place, keep, got, other, mine):
    h = place[4]
    for n in range(2):
        other[n] = (keep[n, 1 - h] + got[n, 1 - h].astype(F32)).astype(BF)
        mine[n] = keep[n, h] + got[n, h].astype(F32)


def head_sum_kernel(place, mine, got, mixed, grad):
    mixed[...] = (mine[0] + got[0].astype(F32)).astype(BF)
    grad[...] = (mine[1] + got[1].astype(F32)).astype(BF)


def scatter_core(place, values, w_out, w):
    local, model = w_out.shape
    shape = (2, 2, local, TOK)
    send, keep = call(
        share_kernel,
        [(shape, BF), (shape, F32)],
        [place, *values, w_out, w],
        [
            pltpu.VMEM((GROUP, HD, TOK), BF),
            pltpu.VMEM((3, GROUP, HD, TOK), BF),
            pltpu.VMEM((model, TOK), F32),
            pltpu.VMEM((4 * HD, TOK), BF),
            pltpu.VMEM(w_out.shape, BF),
            pltpu.VMEM(w.shape, BF),
            pltpu.SemaphoreType.DMA((3,)),
        ],
        mib=18, spaces="shfffhh", out_spaces="ff",
    )
    got = shift(send, "c", 1)
    return call(
        core_sum_kernel, [((2, local, TOK), BF), ((2, local, TOK), F32)], [place, keep, got],
        out_spaces="ff",
    )


def on_device(tokens, w_qkv, w_out, cotangent, block_mask, regions):
    width, model = tokens.shape
    local = w_out.shape[0]
    x = lax.axis_index("x")
    y = lax.axis_index("y")
    row = y * (ROWS // 2) + lax.axis_index("z")
    place = jnp.stack([row, x, y, lax.axis_index("c"), lax.axis_index("h")]).astype(jnp.int32)
    grad_scale = (width * lax.axis_size(SEQ_AXES)) ** (-0.5)
    w2 = w_qkv.transpose(1, 2, 0).reshape(3 * local, model)

    (parts_mine,) = call(
        halves_kernel, [((2, width // 2, model), BF)], [place, tokens, cotangent],
        [pltpu.VMEM((2, width // 2, model), BF), pltpu.SemaphoreType.DMA((4,))],
        spaces="shh", out_spaces="h", moved=4_000_000,
    )
    first, parts_mine = lax.optimization_barrier((tokens, parts_mine))
    sent = call(
        project_kernel,
        [((SENT, width), BF)] * GROUP,
        [place, w2, first, regions, block_mask],
        [
            pltpu.VMEM((3, local, model), BF),
            pltpu.VMEM((width, model), BF),
            pltpu.VMEM(regions.shape, jnp.int32),
            pltpu.VMEM(block_mask.shape, jnp.int32),
            pltpu.VMEM((16, width), F32),
            pltpu.VMEM((3, GROUP, HD, width), BF),
            pltpu.VMEM((GROUP, SENT, width), BF),
            pltpu.SemaphoreType.DMA((12,)),
        ],
        mib=16, spaces="shhhh", out_spaces="fhhh",
        flops=2 * 3 * local * model * width, moved=8_000_000,
    )
    parts = [sent[0]] + [shift(sent[k], "x", k) for k in (1, 2, 3)]
    gathered = lax.all_gather(parts_mine, ("x", "c"), axis=0)
    to_next, to_prev = call(
        halo_kernel, [((2 * HD + 16, HALO), BF)] * 2, [place, *parts], moved=2_000_000
    )
    late_cot, _ = lax.optimization_barrier((cotangent, sent[0]))
    sent_grad = call(
        project_grad_kernel, [((HD, width), BF)] * GROUP, [place, w_out, late_cot],
        [pltpu.VMEM((GROUP, HD, width), BF)], out_spaces="ffff",
        flops=2 * local * model * width, moved=3_000_000,
    )
    to_next, sent_grad = lax.optimization_barrier((to_next, sent_grad))
    grads = [sent_grad[0]] + [shift(sent_grad[k], "x", k) for k in (1, 2, 3)]
    from_prev = shift(to_next, ROW_AXES, 1)
    from_next = shift(to_prev, ROW_AXES, -1)
    held = own_forward(place, parts)
    p1, m1, l1, o1, qn, qt, kt, vt, reg, eff_far = held

    gp, gn, attn, dos1, delta1, dq2 = far_part(
        place, [*grads, eff_far, reg, qn, m1, l1, o1, qt, from_prev, from_next]
    )
    back_next = shift(gp, ROW_AXES, -1)
    back_prev = shift(gn, ROW_AXES, 1)
    dq, own = own_backward(place, [p1, dos1, delta1, dq2, qt, kt, vt])
    d_all, *chunks = call(
        combine_kernel, [((4 * HD, ROW), BF)] + [((4 * HD, width), BF)] * GROUP,
        [place, attn, dq, own, back_next, back_prev],
        [pltpu.VMEM((4 * HD, width), BF), pltpu.SemaphoreType.DMA],
        out_spaces="fhfff",
    )
    kv_all = [chunks[0]] + [shift(chunks[k], "x", k) for k in (1, 2, 3)]
    share = model // ROWS // GROUP
    gathered, d_all = lax.optimization_barrier((gathered, d_all))
    (terms,) = call(
        functools.partial(weights_kernel, grad_scale),
        [((ROWS // 2, 8 * share + 48, MAIN), BF)],
        [place, d_all, gathered],
        [
            pltpu.VMEM((ROW, model), BF),
            pltpu.VMEM((ROW, model), BF),
            pltpu.SemaphoreType.DMA((2, 2 * GROUP)),
        ],
        spaces="svh", out_spaces="f", mib=20,
    )
    spread = lax.all_to_all(terms, "z", 0, 0, tiled=True)
    other, mine = scatter_core(place, kv_all, w_out, w2)
    got = shift(other, "h", 1)
    (summed,) = call(row_sum_kernel, [((2 * GROUP, share, 4 * HD), F32)], [place, spread], out_spaces="f")
    final = lax.all_to_all(summed, ("y", "x"), 0, 0, tiled=True)
    mixed_t, grad_tokens_t = call(head_sum_kernel, [((local, width), BF)] * 2, [place, mine, got])
    final, mixed_t = lax.optimization_barrier((final, mixed_t))
    grad_qkv_t, grad_out_t = call(
        order_kernel, [((3, share, local), F32), ((share, local), F32)], [place, final]
    )
    return (mixed_t.T, grad_tokens_t.T, grad_qkv_t.transpose(1, 0, 2), grad_out_t.T)


def solution(mesh):
    devices = mesh.devices.reshape(2, ROWS // 2, GROUP, 2, 2)
    fine = Mesh(devices, ("y", "z", "x", "h", "c"))
    placed = (
        P(SEQ_AXES, None),
        P(None, None, HEAD_AXES),
        P(HEAD_AXES, None),
        P(SEQ_AXES, None),
        P(SEQ_AXES, None),
        P(SEQ_AXES),
    )
    return jax.shard_map(
        on_device,
        mesh=fine,
        in_specs=placed,
        out_specs=(
            P(SEQ_AXES, HEAD_AXES),
            P(SEQ_AXES, HEAD_AXES),
            P(SEQ_AXES, None, HEAD_AXES),
            P(HEAD_AXES, SEQ_AXES),
        ),
        check_vma=False,
    )
```

```python
import functools

import jax
import jax.numpy as jnp
from jax import lax
from jax.experimental import pallas as pl
from jax.experimental.pallas import tpu as pltpu
from jax.sharding import Mesh
from jax.sharding import PartitionSpec as P

HD = 80
BLOCK = 128
SPAN = 3
TOK = 384
GROUP = 4
PIECES = GROUP + 2 * SPAN
WINDOW = 2 * SPAN + 1
ROW = GROUP * TOK
HALO = SPAN * TOK
KEYS = PIECES * TOK
ROWS = 16
NB = 192
SCALE = HD ** (-0.5)
LOG2E = 1.4426950408889634
NEG = -1e30
BF = jnp.bfloat16
F32 = jnp.float32
MIB = 1024 * 1024
SENT = 3 * HD + 16
WIDE = ROW // 2
MAIN = 256
ROW_AXES = ("y", "z")
SEQ_AXES = ("y", "z", "x")
HEAD_AXES = ("h", "c")


def shift(value, axis, steps):
    count = lax.axis_size(axis)
    return lax.ppermute(value, axis, [(i, (i + steps) % count) for i in range(count)])


def spec_vmem():
    return pl.BlockSpec(memory_space=pltpu.VMEM)


def spec_smem():
    return pl.BlockSpec(memory_space=pltpu.SMEM)


def call(kernel, outs, ins, scratch=(), mib=12, flops=0, moved=0, exps=0, spaces=None, out_spaces=None):
    anywhere = pl.BlockSpec(memory_space=pl.ANY)
    spec = {"v": spec_vmem(), "s": spec_smem(), "a": anywhere, "h": anywhere, "f": spec_vmem()}
    kept = {"h": pltpu.HBM, "f": pltpu.VMEM}
    spaces = spaces or "s" + "v" * (len(ins) - 1)
    out_spaces = out_spaces or "v" * len(outs)
    ins = [pltpu.with_memory_space_constraint(a, kept[c]) if c in kept else a for a, c in zip(ins, spaces)]
    return pl.pallas_call(
        kernel,
        out_shape=[kept.get(c, jax.ShapeDtypeStruct)(s, d) for (s, d), c in zip(outs, out_spaces)],
        in_specs=[spec[c] for c in spaces],
        out_specs=[spec[c] for c in out_spaces],
        scratch_shapes=list(scratch),
        compiler_params=pltpu.CompilerParams(vmem_limit_bytes=mib * MIB),
        cost_estimate=pl.CostEstimate(flops=flops, bytes_accessed=moved, transcendentals=exps),
    )(*ins)


def dot_nn(a, b):
    return lax.dot_general(a, b, (((1,), (0,)), ((), ())), preferred_element_type=F32)


def dot_nt(a, b):
    return lax.dot_general(a, b, (((1,), (1,)), ((), ())), preferred_element_type=F32)


def halves_kernel(place, tokens, cotangent, parts, held, sems):
    half = tokens.shape[0] // 2
    mine = pl.ds(pl.multiple_of(place[3] * half, half), half)
    loads = [pltpu.make_async_copy(a.at[mine], held.at[n], sems.at[n]) for n, a in enumerate((tokens, cotangent))]
    stores = [pltpu.make_async_copy(held.at[n], parts.at[n], sems.at[2 + n]) for n in range(2)]
    for copy in loads:
        copy.start()
    for load, store in zip(loads, stores):
        load.wait()
        store.start()
    for copy in stores:
        copy.wait()


def project_kernel(place, w, tokens, regions, mask, o0, o1, o2, o3, wv, tv, rv, mv, extra, held, stage, sems):
    x = place[1]
    width = tokens.shape[0]
    local = GROUP * HD
    pairs = [(tokens, tv)] + [(w.at[n * local : (n + 1) * local], wv.at[n]) for n in range(3)]
    pairs = pairs + [(regions, rv), (mask, mv)]
    copies = [pltpu.make_async_copy(a, b, sems.at[n]) for n, (a, b) in enumerate(pairs)]
    for copy in copies:
        copy.start()
    outs = []
    copies[0].wait()
    for n in range(3):
        copies[1 + n].wait()
        held[n] = dot_nt(wv[n], tv[...]).astype(BF).reshape(GROUP, HD, width)
    copies[4].wait()
    copies[5].wait()
    extra[...] = jnp.zeros_like(extra)
    extra[0:1, :] = rv[...].reshape(1, -1).astype(F32)
    extra[1:4, :NB] = mv[...].astype(F32)
    for k, out in enumerate((o0, o1, o2, o3)):
        head = lax.rem(x + k, GROUP)
        into = out if k == 0 else stage.at[k]
        for piece in range(3):
            into[piece * HD : (piece + 1) * HD, :] = held[piece, head]
        into[3 * HD :, :] = extra[...].astype(BF)
        if k > 0:
            copy = pltpu.make_async_copy(into, out, sems.at[8 + k])
            copy.start()
            outs.append(copy)
    for copy in outs:
        copy.wait()


def project_grad_kernel(place, w_out, cotangent, o0, o1, o2, o3, held):
    x = place[1]
    held[...] = dot_nt(w_out[...], cotangent[...]).astype(BF).reshape(GROUP, HD, -1)
    for k, out in enumerate((o0, o1, o2, o3)):
        out[...] = held[lax.rem(x + k, GROUP)]


def dot_tn(a, b):
    return lax.dot_general(a, b, (((0,), (0,)), ((), ())), preferred_element_type=F32)


def halo_kernel(place, r0, r1, r2, r3, to_next, to_prev):
    x = place[1]
    for k, ref in enumerate((r0, r1, r2, r3)):
        pos = lax.rem(x - k + GROUP, GROUP)

        @pl.when(pos >= 1)
        def _():
            at = pl.multiple_of((pos - 1) * TOK, TOK)
            to_next[:, pl.ds(at, TOK)] = ref[HD : 3 * HD + 16, :]

        @pl.when(pos <= 2)
        def _():
            at = pl.multiple_of(pos * TOK, TOK)
            to_prev[:, pl.ds(at, TOK)] = ref[HD : 3 * HD + 16, :]


def block_rows(i):
    return slice(i * BLOCK, (i + 1) * BLOCK)


def open_regions(eff, key_reg, first, i):
    opened = eff > 0.5
    if first is not None:
        blocks = lax.broadcasted_iota(jnp.int32, eff.shape, 1) // BLOCK
        opened = opened | (blocks == first + i)
    return jnp.where(opened, key_reg, -1.0)


def lane_sum(p):
    total = p[:, :BLOCK]
    for g in range(1, p.shape[1] // BLOCK):
        total = total + p[:, g * BLOCK : (g + 1) * BLOCK]
    return jnp.sum(total, axis=1, keepdims=True)


def lane_max(s):
    top = s[:, :BLOCK]
    for g in range(1, s.shape[1] // BLOCK):
        top = jnp.maximum(top, s[:, g * BLOCK : (g + 1) * BLOCK])
    return jnp.max(top, axis=1, keepdims=True)


def own_forward_kernel(place, r0, r1, r2, r3,
                       p1, m1, l1, o1, qn, qt, kt, vt, reg, eff_far,
                       eff_own, s_ref):
    row = place[0]
    x = place[1]
    lane = lax.broadcasted_iota(jnp.int32, (256, KEYS), 1) // BLOCK
    per_row = ROW // BLOCK
    per_halo = HALO // BLOCK
    ahead = jnp.where(lane < per_row, lane, jnp.where(lane < per_row + per_halo, lane - per_row - per_halo, lane - per_halo))
    block_id = lax.rem(ahead + row * per_row + NB, NB)
    pick = jnp.where(block_id == lax.broadcasted_iota(jnp.int32, (256, KEYS), 0), 1.0, 0.0).astype(BF)
    for k, ref in enumerate((r0, r1, r2, r3)):
        pos = lax.rem(x - k + GROUP, GROUP)
        cols = pl.ds(pl.multiple_of(pos * TOK, TOK), TOK)
        extra = ref[3 * HD : 3 * HD + 16, :]
        eff = dot_nn(extra[:, :256], pick)
        eff_own[pos] = eff[:, :ROW]
        eff_far[pos] = eff[:, ROW:]
        reg[:, cols] = extra.astype(F32)
        qt[:, cols] = ref[:HD, :]
        kt[:, cols] = ref[HD : 2 * HD, :]
        vt[:, cols] = ref[2 * HD : 3 * HD, :]
        qn[pos] = ref[:HD, :].astype(F32).T.astype(BF)

    tops = []
    for r in range(GROUP):
        rows = slice(r * TOK, (r + 1) * TOK)
        reg_q = reg[:, rows].T[:, 0:1]
        raw = dot_nn(qn[r], kt[...])
        top = []
        for i in range(3):
            key_eff = open_regions(eff_own[r, 1 + i : 2 + i, :], reg[0:1, :], 3 * r, i)
            s = jnp.where(reg_q[block_rows(i)] == key_eff, raw[block_rows(i)], NEG)
            s_ref[r, block_rows(i), :] = s
            top.append(lane_max(s))
        tops.append(jnp.concatenate(top, axis=0))
        m1[r] = tops[r]
    for r in range(GROUP):
        rows = slice(r * TOK, (r + 1) * TOK)
        p = jnp.exp2((s_ref[r] - tops[r]) * (SCALE * LOG2E))
        p1[rows, :] = p.astype(BF)
        l1[r] = lane_sum(p)
        o1[r] = dot_nt(p1[rows, :], vt[...])


def far_kernel(place, d0, d1, d2, d3, eff_far, reg, qn, m1, l1, o1, qt, from_prev, from_next,
               gp, gn, attn, dos1, delta1, dq2,
               kh, vh, regh, s_ref, p_ref, ds_ref, dk, dv, don):
    x = place[1]
    for k, ref in enumerate((d0, d1, d2, d3)):
        don[lax.rem(x - k + GROUP, GROUP)] = ref[...].astype(F32).T
    for ref, cols in ((from_prev, slice(0, HALO)), (from_next, slice(HALO, 2 * HALO))):
        kh[:, cols] = ref[:HD, :]
        vh[:, cols] = ref[HD : 2 * HD, :]
        regh[:, cols] = ref[2 * HD :, :].astype(F32)
    dk[...] = jnp.zeros_like(dk)
    dv[...] = jnp.zeros_like(dv)

    tops = []
    for r in range(GROUP):
        rows = slice(r * TOK, (r + 1) * TOK)
        win = slice(r * TOK, r * TOK + HALO)
        reg_q = reg[:, rows].T[:, 0:1]
        raw = dot_nn(qn[r], kh[:, win])
        top = []
        for i in range(3):
            key_eff = open_regions(eff_far[r, 1 + i : 2 + i, win], regh[0:1, win], None, i)
            s = jnp.where(reg_q[block_rows(i)] == key_eff, raw[block_rows(i)], NEG)
            s_ref[r, block_rows(i), :] = s
            top.append(lane_max(s))
        tops.append(jnp.maximum(jnp.concatenate(top, axis=0), 0.1 * NEG))
    held = []
    for r in range(GROUP):
        win = slice(r * TOK, r * TOK + HALO)
        p = jnp.exp2((s_ref[r] - tops[r]) * (SCALE * LOG2E))
        p_ref[r] = p.astype(BF)
        held.append((lane_sum(p), dot_nt(p_ref[r], vh[:, win])))
    stats = []
    for r in range(GROUP):
        rows = slice(r * TOK, (r + 1) * TOK)
        m2 = tops[r]
        l2, o2 = held[r]
        m = jnp.maximum(m1[r], m2)
        w1 = jnp.exp2((m1[r] - m) * (SCALE * LOG2E))
        w2 = jnp.exp2((m2 - m) * (SCALE * LOG2E))
        inv = 1.0 / (l1[r] * w1 + l2 * w2)
        w1 = w1 * inv
        w2 = w2 * inv
        at_n = (o1[r] * w1 + o2 * w2).astype(BF).astype(F32)
        do_n = don[r]
        near = (do_n * (w1 * SCALE)).astype(BF)
        far = (do_n * (w2 * SCALE)).astype(BF)
        dos1[rows, :] = near
        delta1[r] = jnp.sum(near.astype(F32) * at_n, axis=1, keepdims=True)
        attn[:, rows] = at_n.T.astype(BF)
        stats.append((far, jnp.sum(far.astype(F32) * at_n, axis=1, keepdims=True)))
    for r in range(GROUP):
        rows = slice(r * TOK, (r + 1) * TOK)
        win = slice(r * TOK, r * TOK + HALO)
        far, delta2 = stats[r]
        dp = dot_nn(far, vh[:, win])
        ds_ref[r] = (p_ref[r].astype(F32) * (dp - delta2)).astype(BF)
        dq2[r] = dot_nt(ds_ref[r], kh[:, win])
    for r in range(GROUP):
        rows = slice(r * TOK, (r + 1) * TOK)
        win = slice(r * TOK, r * TOK + HALO)
        dk[:, win] += dot_nn(qt[:, rows], ds_ref[r])
        dv[:, win] += dot_nn(stats[r][0].astype(F32).T.astype(BF), p_ref[r])
    for out, cols in ((gp, slice(0, HALO)), (gn, slice(HALO, 2 * HALO))):
        out[:HD, :] = dk[:, cols].astype(BF)
        out[HD:, :] = (dv[:, cols] * (1.0 / SCALE)).astype(BF)


def own_backward_kernel(place, p1, dos1, delta1, dq2, qt, kt, vt, dq, own, ds_ref):
    def step(r, carry):
        rows = pl.ds(pl.multiple_of(r * TOK, TOK), TOK)
        d_q = dq2[r]
        near = dos1[rows, :]
        for c in range(2):
            cols = slice(c * WIDE, (c + 1) * WIDE)
            dp = dot_nn(near, vt[:, cols])
            ds = (p1[rows, cols].astype(F32) * (dp - delta1[r])).astype(BF)
            ds_ref[rows, cols] = ds
            d_q = d_q + dot_nt(ds, kt[:, cols])
        dq[:, rows] = d_q.T.astype(BF)
        return carry

    lax.fori_loop(0, GROUP, step, 0, unroll=True)
    dos_t = dos1[...].astype(F32).T.astype(BF)
    for c in range(2):
        cols = slice(c * WIDE, (c + 1) * WIDE)
        own[:HD, cols] = dot_nn(qt[...], ds_ref[:, cols])
        own[HD:, cols] = dot_nn(dos_t, p1[:, cols]) * (1.0 / SCALE)


def own_forward(place, parts):
    stat = ((GROUP, TOK, 1), F32)
    wide = ((GROUP, TOK, HD), F32)
    flat = ((HD, ROW), BF)
    outs = [((ROW, ROW), BF), stat, stat, wide, ((GROUP, TOK, HD), BF), flat, flat, flat]
    outs = outs + [((16, ROW), F32), ((GROUP, 16, 2 * HALO), F32)]
    return call(
        own_forward_kernel, outs, [place, *parts],
        [pltpu.VMEM((GROUP, 16, ROW), F32), pltpu.VMEM((GROUP, TOK, ROW), F32)],
        mib=24, out_spaces="f" * len(outs),
        flops=4 * ROW * ROW * 128, moved=6_000_000, exps=ROW * ROW,
    )


def far_part(place, ins):
    outs = [((2 * HD, HALO), BF)] * 2 + [((HD, ROW), BF), ((ROW, HD), BF), ((GROUP, TOK, 1), F32)]
    outs = outs + [((GROUP, TOK, HD), F32)]
    scratch = [
        pltpu.VMEM((HD, 2 * HALO), BF),
        pltpu.VMEM((HD, 2 * HALO), BF),
        pltpu.VMEM((16, 2 * HALO), F32),
        pltpu.VMEM((GROUP, TOK, HALO), F32),
        pltpu.VMEM((GROUP, TOK, HALO), BF),
        pltpu.VMEM((GROUP, TOK, HALO), BF),
        pltpu.VMEM((HD, 2 * HALO), F32),
        pltpu.VMEM((HD, 2 * HALO), F32),
        pltpu.VMEM((GROUP, TOK, HD), F32),
    ]
    return call(
        far_kernel, outs, [place, *ins], scratch, mib=28, out_spaces="f" * len(outs),
        flops=12 * ROW * HALO * 128, moved=6_000_000, exps=ROW * HALO,
    )


def own_backward(place, ins):
    return call(
        own_backward_kernel, [((HD, ROW), BF), ((2 * HD, ROW), F32)], [place, *ins],
        [pltpu.VMEM((ROW, ROW), BF)], mib=24, out_spaces="ff",
        flops=8 * ROW * ROW * 128, moved=6_000_000,
    )


def combine_kernel(place, attn, dq, own, from_next, from_prev, full, c0, c1, c2, c3, stage, sem):
    x = place[1]
    full[:HD, :] = attn[...]
    full[HD : 2 * HD, :] = dq[...]
    full[2 * HD :, :TOK] = (own[:, :TOK] + from_prev[:, :TOK].astype(F32)).astype(BF)
    middle = own[:, TOK:HALO] + from_next[:, : HALO - TOK].astype(F32)
    full[2 * HD :, TOK:HALO] = (middle + from_prev[:, TOK:].astype(F32)).astype(BF)
    full[2 * HD :, HALO:] = (own[:, HALO:] + from_next[:, HALO - TOK :].astype(F32)).astype(BF)
    for k, out in enumerate((stage, c1, c2, c3)):
        at = pl.multiple_of(lax.rem(x + k, GROUP) * TOK, TOK)
        out[...] = full[:, pl.ds(at, TOK)]
        if k == 0:
            copy = pltpu.make_async_copy(stage, c0, sem)
            copy.start()
    copy.wait()


def weights_kernel(scale, place, values, gathered, out, tokens, cotangent, sems):
    parts, _, part_rows, _ = gathered.shape
    copies = []
    for which, into in ((1, cotangent), (0, tokens)):
        for n in range(parts):
            to = into.at[n * part_rows : (n + 1) * part_rows]
            copies.append(pltpu.make_async_copy(gathered.at[n, which], to, sems.at[which, n]))
    for copy in copies:
        copy.start()
    for copy in copies[:parts]:
        copy.wait()
    first = dot_nn(values[:HD, :], cotangent[...])
    for copy in copies[parts:]:
        copy.wait()
    total = (jnp.concatenate([first, dot_nn(values[HD:, :], tokens[...])], axis=0) * scale).T
    count = out.shape[0]
    rows = total.shape[0] // (2 * count)
    for z in range(count):
        first = total[z * rows : (z + 1) * rows]
        second = total[(count + z) * rows : (count + z + 1) * rows]
        both = jnp.concatenate([first, second], axis=0)
        out[z, : 2 * rows, :] = both[:, :MAIN].astype(BF)
        fold = rows // 2
        rest = [both[g * fold : (g + 1) * fold, MAIN:] for g in range(4)]
        folded = jnp.concatenate([jnp.concatenate(rest, axis=1), jnp.zeros((8, MAIN), F32)], axis=0)
        out[z, 2 * rows :, :] = folded.astype(BF)


def row_sum_kernel(place, spread, out):
    total = jnp.sum(spread[...].astype(F32), axis=0)
    count, share, _ = out.shape
    rest = count * share
    for n in range(count):
        at = rest + (n % 2) * share
        left = (n // 2) * (4 * HD - MAIN)
        out[n, :, :MAIN] = total[n * share : (n + 1) * share].astype(BF)
        out[n, :, MAIN:] = total[at : at + share, left : left + 4 * HD - MAIN].astype(BF)


def order_kernel(place, final, grad_qkv, grad_out):
    for h in range(GROUP):
        piece = final[h].astype(F32) + final[GROUP + h].astype(F32)
        cols = slice(h * HD, (h + 1) * HD)
        grad_out[:, cols] = piece[:, :HD]
        for part in range(3):
            grad_qkv[part, :, cols] = piece[:, (part + 1) * HD : (part + 2) * HD]


def share_kernel(place, mine, r1, r2, r3, w_out, w, send, keep, attn, grads, whole, mv, wov, wv, sems):
    pairs = ((mine, mv), (w_out, wov), (w, wv))
    copies = [pltpu.make_async_copy(a, b, sems.at[n]) for n, (a, b) in enumerate(pairs)]
    for copy in copies:
        copy.start()
    x = place[1]
    core = place[3]
    for k, ref in enumerate((r1, r2, r3, mv)):
        if ref is mv:
            copies[0].wait()
        head = lax.rem(x - (k + 1) + GROUP, GROUP)
        attn[head] = ref[:HD, :]
        for part in range(3):
            grads[part, head] = ref[(part + 1) * HD : (part + 2) * HD, :]
    local = GROUP * HD
    for n, (weights, held) in enumerate(((wov, attn), (wv, grads))):
        copies[n + 1].wait()
        values = held[...].reshape(-1, TOK)
        whole[...] = dot_tn(weights[...], values)
        for other, out in ((1, send), (0, keep)):
            for h in range(2):
                at = pl.multiple_of((2 * h + lax.rem(core + other, 2)) * local, local)
                out[n, h] = whole[pl.ds(at, local), :].astype(out.dtype)


def core_sum_kernel(place, keep, got, other, mine):
    h = place[4]
    for n in range(2):
        other[n] = (keep[n, 1 - h] + got[n, 1 - h].astype(F32)).astype(BF)
        mine[n] = keep[n, h] + got[n, h].astype(F32)


def head_sum_kernel(place, mine, got, mixed, grad):
    mixed[...] = (mine[0] + got[0].astype(F32)).astype(BF)
    grad[...] = (mine[1] + got[1].astype(F32)).astype(BF)


def scatter_core(place, values, w_out, w):
    local, model = w_out.shape
    shape = (2, 2, local, TOK)
    send, keep = call(
        share_kernel,
        [(shape, BF), (shape, F32)],
        [place, *values, w_out, w],
        [
            pltpu.VMEM((GROUP, HD, TOK), BF),
            pltpu.VMEM((3, GROUP, HD, TOK), BF),
            pltpu.VMEM((model, TOK), F32),
            pltpu.VMEM((4 * HD, TOK), BF),
            pltpu.VMEM(w_out.shape, BF),
            pltpu.VMEM(w.shape, BF),
            pltpu.SemaphoreType.DMA((3,)),
        ],
        mib=18, spaces="shfffhh", out_spaces="ff",
    )
    got = shift(send, "c", 1)
    return call(
        core_sum_kernel, [((2, local, TOK), BF), ((2, local, TOK), F32)], [place, keep, got],
        out_spaces="ff",
    )


def on_device(tokens, w_qkv, w_out, cotangent, block_mask, regions):
    width, model = tokens.shape
    local = w_out.shape[0]
    x = lax.axis_index("x")
    y = lax.axis_index("y")
    row = y * (ROWS // 2) + lax.axis_index("z")
    place = jnp.stack([row, x, y, lax.axis_index("c"), lax.axis_index("h")]).astype(jnp.int32)
    grad_scale = (width * lax.axis_size(SEQ_AXES)) ** (-0.5)
    w2 = w_qkv.transpose(1, 2, 0).reshape(3 * local, model)

    (parts_mine,) = call(
        halves_kernel, [((2, width // 2, model), BF)], [place, tokens, cotangent],
        [pltpu.VMEM((2, width // 2, model), BF), pltpu.SemaphoreType.DMA((4,))],
        spaces="shh", out_spaces="h", moved=4_000_000,
    )
    first, parts_mine = lax.optimization_barrier((tokens, parts_mine))
    sent = call(
        project_kernel,
        [((SENT, width), BF)] * GROUP,
        [place, w2, first, regions, block_mask],
        [
            pltpu.VMEM((3, local, model), BF),
            pltpu.VMEM((width, model), BF),
            pltpu.VMEM(regions.shape, jnp.int32),
            pltpu.VMEM(block_mask.shape, jnp.int32),
            pltpu.VMEM((16, width), F32),
            pltpu.VMEM((3, GROUP, HD, width), BF),
            pltpu.VMEM((GROUP, SENT, width), BF),
            pltpu.SemaphoreType.DMA((12,)),
        ],
        mib=16, spaces="shhhh", out_spaces="fhhh",
        flops=2 * 3 * local * model * width, moved=8_000_000,
    )
    parts = [sent[0]] + [shift(sent[k], "x", k) for k in (1, 2, 3)]
    gathered = lax.all_gather(parts_mine, ("x", "c"), axis=0)
    to_next, to_prev = call(
        halo_kernel, [((2 * HD + 16, HALO), BF)] * 2, [place, *parts], moved=2_000_000
    )
    late_cot, _ = lax.optimization_barrier((cotangent, sent[0]))
    sent_grad = call(
        project_grad_kernel, [((HD, width), BF)] * GROUP, [place, w_out, late_cot],
        [pltpu.VMEM((GROUP, HD, width), BF)], out_spaces="ffff",
        flops=2 * local * model * width, moved=3_000_000,
    )
    to_next, sent_grad = lax.optimization_barrier((to_next, sent_grad))
    grads = [sent_grad[0]] + [shift(sent_grad[k], "x", k) for k in (1, 2, 3)]
    from_prev = shift(to_next, ROW_AXES, 1)
    from_next = shift(to_prev, ROW_AXES, -1)
    held = own_forward(place, parts)
    p1, m1, l1, o1, qn, qt, kt, vt, reg, eff_far = held

    gp, gn, attn, dos1, delta1, dq2 = far_part(
        place, [*grads, eff_far, reg, qn, m1, l1, o1, qt, from_prev, from_next]
    )
    back_next = shift(gp, ROW_AXES, -1)
    back_prev = shift(gn, ROW_AXES, 1)
    dq, own = own_backward(place, [p1, dos1, delta1, dq2, qt, kt, vt])
    d_all, *chunks = call(
        combine_kernel, [((4 * HD, ROW), BF)] + [((4 * HD, width), BF)] * GROUP,
        [place, attn, dq, own, back_next, back_prev],
        [pltpu.VMEM((4 * HD, width), BF), pltpu.SemaphoreType.DMA],
        out_spaces="fhfff",
    )
    kv_all = [chunks[0]] + [shift(chunks[k], "x", k) for k in (1, 2, 3)]
    share = model // ROWS // GROUP
    gathered, d_all = lax.optimization_barrier((gathered, d_all))
    (terms,) = call(
        functools.partial(weights_kernel, grad_scale),
        [((ROWS // 2, 8 * share + 48, MAIN), BF)],
        [place, d_all, gathered],
        [
            pltpu.VMEM((ROW, model), BF),
            pltpu.VMEM((ROW, model), BF),
            pltpu.SemaphoreType.DMA((2, 2 * GROUP)),
        ],
        spaces="svh", out_spaces="f", mib=20,
    )
    spread = lax.all_to_all(terms, "z", 0, 0, tiled=True)
    other, mine = scatter_core(place, kv_all, w_out, w2)
    got = shift(other, "h", 1)
    (summed,) = call(row_sum_kernel, [((2 * GROUP, share, 4 * HD), BF)], [place, spread], out_spaces="f")
    final = lax.all_to_all(summed, ("y", "x"), 0, 0, tiled=True)
    mixed_t, grad_tokens_t = call(head_sum_kernel, [((local, width), BF)] * 2, [place, mine, got])
    final, mixed_t = lax.optimization_barrier((final, mixed_t))
    grad_qkv_t, grad_out_t = call(
        order_kernel, [((3, share, local), F32), ((share, local), F32)], [place, final]
    )
    return (mixed_t.T, grad_tokens_t.T, grad_qkv_t.transpose(1, 0, 2), grad_out_t.T)


def solution(mesh):
    devices = mesh.devices.reshape(2, ROWS // 2, GROUP, 2, 2)
    fine = Mesh(devices, ("y", "z", "x", "h", "c"))
    placed = (
        P(SEQ_AXES, None),
        P(None, None, HEAD_AXES),
        P(HEAD_AXES, None),
        P(SEQ_AXES, None),
        P(SEQ_AXES, None),
        P(SEQ_AXES),
    )
    return jax.shard_map(
        on_device,
        mesh=fine,
        in_specs=placed,
        out_specs=(
            P(SEQ_AXES, HEAD_AXES),
            P(SEQ_AXES, HEAD_AXES),
            P(SEQ_AXES, None, HEAD_AXES),
            P(HEAD_AXES, SEQ_AXES),
        ),
        check_vma=False,
    )
```
